128 devices in a mesh: gx: 4 (over z_lo, core), gy: 8 (over y, z_hi), gz: 4 (over x).
Axes of the slice: x: 4, y: 4, z: 4 (z_hi: 2, z_lo: 2; z = z_hi * 2 + z_lo), core: 2. Of those that a mesh axis runs over, the one named last changes fastest.
Arguments:
- saved: float32 [3, 27, 32, 64, 512], P(None, None, 'gx', 'gy', 'gz'), may hold values from 0.02 to 0.08
- porosity: float32 [32, 64, 512], P('gx', 'gy', 'gz'), may hold values from 0.05 to 0.6
- fluid: int32 [32, 64, 512], P('gx', 'gy', 'gz'), may hold values 0 or 1
- seed_adjoint: float32 [27, 32, 64, 512], P(None, 'gx', 'gy', 'gz'), may hold values from -6 to 6
Outputs:
- adjoint_first: float32 [27, 32, 64, 512], P(None, 'gx', 'gy', 'gz')
- porosity_grad: float32 [32, 64, 512], P('gx', 'gy', 'gz')
The draws below stay inside these ranges and needn't reach their ends.
All inputs are finite; a program needn't handle non-finite values. No bound on the sum of `fluid` on one device may be relied on, other than what follows from the above.
Results may differ from the reference program's by a relative error of at most 0.0001.
Values sent between devices are 32-bit elements; how exact they have to be, the bound alone decides.
A program may use at most 64 MiB of HBM per device.

```python
import jax
import jax.numpy as jnp
import numpy as np
from jax import lax

Q = 27
STEPS = 3
NX = 32
NY = 64
NZ = 512


def plant(result, own_key, low, largest):
    longest = result.shape.index(max(result.shape))
    spots = []
    for shift in (0, 1):
        where = [jax.random.randint(jax.random.fold_in(own_key, axis), (), 0, length) for axis, length in enumerate(result.shape)]
        where[longest] = (where[longest] + shift) % result.shape[longest]
        spots.append(tuple(where))
    return result.at[spots[0]].set(low).at[spots[1]].set(largest)


def level_of(key, extent, split, smallest, largest):
    loudness, own = 1.0, jax.random.fold_in(key, 6)
    for position, blocks in split:
        heights = jnp.exp(jax.random.uniform(jax.random.fold_in(own, position), (blocks,), jnp.float32, smallest / len(split), largest / len(split)))
        loudness = loudness * jnp.repeat(heights, extent[position] // blocks).reshape([-1 if axis == position else 1 for axis in range(len(extent))])
    return loudness


def normal_values(own_key, extent, scale, reach, cuts=(), kind=jnp.bfloat16):
    drawn = scale * jax.random.normal(own_key, extent, jnp.float32)
    if cuts:
        drawn = drawn * level_of(own_key, extent, cuts, -0.22, 0.18)
    return jnp.clip(drawn, -reach, reach).astype(kind)


def setup_inputs(seed: int = 0) -> dict:
    arg_keys = jax.random.split(jax.random.key(seed), 5)
    saved = jnp.clip(0.02 + 0.06 * jax.random.uniform(arg_keys[0], (STEPS, Q, NX, NY, NZ), jnp.float32) ** level_of(arg_keys[0], (STEPS, Q, NX, NY, NZ), ((2, 4), (3, 8), (4, 4)), -0.2, 0.2), 0.02, 0.08)
    porosity = jnp.clip(0.05 + 0.55 * jax.random.uniform(arg_keys[1], (NX, NY, NZ), jnp.float32) ** level_of(arg_keys[1], (NX, NY, NZ), ((0, 4), (1, 8), (2, 4)), -0.2, 0.2), 0.05, 0.6)
    fluid = plant((jax.random.randint(arg_keys[2], (NX, NY, NZ), 0, 8) < 7).astype(jnp.int32), jax.random.fold_in(arg_keys[2], 1), 0, 1)
    seed_adjoint = normal_values(arg_keys[3], (Q, NX, NY, NZ), 1.0, 6.0, ((1, 4), (2, 8), (3, 4)), jnp.float32)
    return dict(saved=saved, porosity=porosity, fluid=fluid, seed_adjoint=seed_adjoint)


def lattice():
    vel = np.array([[a, b, c] for a in (-1, 0, 1) for b in (-1, 0, 1) for c in (-1, 0, 1)], dtype=np.int64)
    nonzero = np.abs(vel).sum(axis=1)
    table = np.array([8.0 / 27, 2.0 / 27, 1.0 / 54, 1.0 / 216])
    return (vel, table[nonzero])

def collide(pops, porosity, fluid):
    vel, weights = lattice()
    shape = (27, 1, 1, 1)
    vx = jnp.asarray(vel[:, 0].reshape(shape), jnp.float32)
    vy = jnp.asarray(vel[:, 1].reshape(shape), jnp.float32)
    vz = jnp.asarray(vel[:, 2].reshape(shape), jnp.float32)
    wts = jnp.asarray(weights.reshape(shape), jnp.float32)
    solid = jnp.where(fluid == 1, porosity, jnp.ones_like(porosity))
    density = lax.optimization_barrier(jnp.sum(pops, axis=0))
    ux = lax.optimization_barrier(jnp.sum(pops * vx, axis=0)) / density
    uy = lax.optimization_barrier(jnp.sum(pops * vy, axis=0)) / density
    uz = lax.optimization_barrier(jnp.sum(pops * vz, axis=0)) / density
    cu = vx * ux + vy * uy + vz * uz
    usq = ux * ux + uy * uy + uz * uz
    equil = wts * density * (1.0 + 3.0 * cu + 4.5 * cu * cu - 1.5 * usq)
    relaxed = pops - 1.6 * (pops - equil)
    return (1.0 - solid) * relaxed + solid * pops[::-1]

def pull(adjoint):
    vel, weights = lattice()
    nx, ny, nz = (adjoint.shape[1], adjoint.shape[2], adjoint.shape[3])
    padded = jnp.pad(adjoint, ((0, 0), (1, 1), (1, 1), (1, 1)))
    pieces = []
    for index in range(27):
        ax, ay, az = (int(vel[index, 0]) + 1, int(vel[index, 1]) + 1, int(vel[index, 2]) + 1)
        pieces.append(padded[index, ax:ax + nx, ay:ay + ny, az:az + nz])
    return jnp.stack(pieces, axis=0)

def reference(saved, porosity, fluid, seed_adjoint):
    adjoint = seed_adjoint
    grad = jnp.zeros(porosity.shape, jnp.float32)
    for step in range(STEPS - 1, -1, -1):
        pulled = pull(adjoint)
        outputs, backward = jax.vjp(lambda pops, poro: collide(pops, poro, fluid), saved[step], porosity)
        adjoint, term = backward(pulled)
        grad = grad + term
    return (adjoint, grad)
```

```python
import functools
import itertools

import jax
import jax.numpy as jnp
from jax import lax
from jax.experimental import pallas as pl
from jax.experimental.pallas import tpu as pltpu
from jax.sharding import PartitionSpec as P

STEPS = 3
AXES = ("gx", "gy", "gz")
OFFSETS = sorted(
    (o for o in itertools.product((-1, 0, 1), repeat=3) if any(o)),
    key=lambda o: (o[2] != 0, sum(map(abs, o)), o[0] != 0),
)
PAIRS = tuple(itertools.product(range(3), range(3)))


def f_moments(pops):
    s = [[pops(a, b, 0) + pops(a, b, 1) + pops(a, b, 2) for b in range(3)] for a in range(3)]
    dz = [sum(pops(a, b, 2) - pops(a, b, 0) for b in range(3)) for a in range(3)]
    sy = [s[a][0] + s[a][1] + s[a][2] for a in range(3)]
    dy = [s[a][2] - s[a][0] for a in range(3)]
    return (
        sy[0] + sy[1] + sy[2],
        sy[2] - sy[0],
        dy[0] + dy[1] + dy[2],
        dz[0] + dz[1] + dz[2],
    )


def even(v):
    side = v[0] + v[2]
    return 4.0 * v[1] + side, v[2] - v[0], side


def weighted_moments(p):
    z = [[even([p[a][b][c] for c in range(3)]) for b in range(3)] for a in range(3)]
    y = []
    for a in range(3):
        z0, z1, z2 = ([z[a][b][k] for b in range(3)] for k in range(3))
        y00, y10, y20 = even(z0)
        y01, y11, _ = even(z1)
        y02, _, _ = even(z2)
        y.append((y00, y10, y20, y01, y11, y02))
    p0, px, pxx = even([y[a][0] for a in range(3)])
    py, pxy, _ = even([y[a][1] for a in range(3)])
    pyy, _, _ = even([y[a][2] for a in range(3)])
    pz, pxz, _ = even([y[a][3] for a in range(3)])
    pyz, _, _ = even([y[a][4] for a in range(3)])
    pzz, _, _ = even([y[a][5] for a in range(3)])
    return p0, (px, py, pz), (pxx, pyy, pzz, pxy, pxz, pyz)


def kernel(
    sizes, saved, poro, fluid, seed, out, grad,
    adj, pops, flow, por, flu, res, acc, ztile, zrecv,
    lsem, osem, ssem, rsem,
):
    me = [lax.axis_index(a) for a in AXES]

    def exists(off):
        found = None
        for i, o in enumerate(off):
            if o:
                here = me[i] < sizes[i] - 1 if o > 0 else me[i] > 0
                found = here if found is None else jnp.logical_and(found, here)
        return found

    def device(off):
        return tuple(m + o for m, o in zip(me, off))

    def back(off):
        return tuple(-o for o in off)

    loads = [pltpu.make_async_copy(seed, adj.at[0, :, :, :, pl.ds(1, 8), pl.ds(8, 8), :], lsem.at[0])]
    loads += [pltpu.make_async_copy(saved.at[t], pops.at[t], lsem.at[1 + t]) for t in range(STEPS)]
    loads += [pltpu.make_async_copy(poro, por, lsem.at[4]), pltpu.make_async_copy(fluid, flu, lsem.at[5])]

    barrier = pltpu.get_barrier_semaphore()
    count = jnp.int32(0)
    for off in OFFSETS:
        there = exists(off)

        @pl.when(there)
        def _():
            pl.semaphore_signal(barrier, inc=1, device_id=device(off), device_id_type=pl.DeviceIdType.MESH)

        count = count + there.astype(jnp.int32)

    for i in (0, 3, 2, 1, 4, 5):
        loads[i].start()

    zero = jnp.zeros((8, 128), jnp.float32)
    for off in ((-1, 0, 0), (1, 0, 0)):

        @pl.when(jnp.logical_not(exists(off)))
        def _():
            part = 0 if off[0] < 0 else 9

            def clear(r, _):
                for b, c in PAIRS:
                    for tile in range(3):
                        adj[r, 1 + off[0], b, c, part, pl.ds(8 * tile, 8), :] = zero
                return 0

            lax.fori_loop(0, STEPS, clear, 0)

    for off in ((0, -1, 0), (0, 1, 0)):

        @pl.when(jnp.logical_not(exists(off)))
        def _():
            def clear(n, _):
                r, x = n // 10, n % 10
                for a, c in PAIRS:
                    row = 0 if off[1] < 0 else 16
                    adj[r, a, 1 + off[1], c, x, pl.ds(row, 8), :] = zero
                return 0

            lax.fori_loop(0, STEPS * 10, clear, 0)

    for k, off in enumerate(OFFSETS):
        if off[2]:

            @pl.when(jnp.logical_not(exists(back(off))))
            def _():
                for r in range(STEPS):
                    zrecv[r, k] = zero

    lane = lax.broadcasted_iota(jnp.int32, (8, 128), 1)
    row = lax.broadcasted_iota(jnp.int32, (8, 128), 0)
    group = lane >> 3
    inner = lane & 7
    ymod = jnp.where(group < 3, group, jnp.where(group < 6, group - 3, group - 6))
    xmask = {1: (group < 3) & (inner == 0), -1: (group >= 6) & (inner == 7)}
    ymask = {1: (ymod == 0) & (row == 0), -1: (ymod == 2) & (row == 7)}

    def copies(r):
        made = {}
        for k, (dx, dy, dz) in enumerate(OFFSETS):
            a, b = 1 - dx, 1 - dy
            xs, xd = (8, 0) if dx > 0 else (1, 9)
            ys, yd = (15, 7) if dy > 0 else (8, 16)
            if dz:
                src, dst = ztile.at[r, (1 - dz) // 2], zrecv.at[r, k]
            elif not dx:
                src = adj.at[r, :, b, :, pl.ds(1, 8), pl.ds(ys, 1), :]
                dst = adj.at[r, :, b, :, pl.ds(1, 8), pl.ds(yd, 1), :]
            elif not dy:
                src = adj.at[r, a, :, :, xs, pl.ds(8, 8), :]
                dst = adj.at[r, a, :, :, xd, pl.ds(8, 8), :]
            else:
                src = adj.at[r, a, b, :, xs, pl.ds(ys, 1), :]
                dst = adj.at[r, a, b, :, xd, pl.ds(yd, 1), :]
            off = (dx, dy, dz)
            made[off] = pltpu.make_async_remote_copy(
                src, dst, ssem.at[r, k], rsem.at[r, k],
                device_id=device(off), device_id_type=pl.DeviceIdType.MESH,
            )
        return made

    def pack(tiles, x, value):
        lower, upper = tiles
        for a, b in PAIRS:
            spot = (3 * a + b) * 8 + ((x + 1 - a) & 7)
            here = lane == spot
            upper = jnp.where(here, pltpu.roll(value(a, b, 0), spot + 1, 1), upper)
            lower = jnp.where(here, pltpu.roll(value(a, b, 2), spot, 1), lower)
        return lower, upper

    def shifted(tile):
        return jnp.where(ymod == 1, tile, jnp.where(ymod == 0, pltpu.roll(tile, 1, 0), pltpu.roll(tile, 7, 0)))

    def start(r, tiles):
        ztile[r, 1] = shifted(tiles[0])
        ztile[r, 0] = shifted(tiles[1])
        made = copies(r)
        for off in OFFSETS:
            pl.when(exists(off))(made[off].start)

    def arrive(r):
        made = copies(r)
        for off in OFFSETS:
            pl.when(exists(back(off)))(made[off].wait_recv)

    def edge(r, dz):
        def at(dx, dy):
            return zrecv[r, OFFSETS.index((dx, dy, dz))]

        def line(dx):
            return jnp.where(ymask[1], at(dx, 1), jnp.where(ymask[-1], at(dx, -1), at(dx, 0)))

        return jnp.where(xmask[1], line(1), jnp.where(xmask[-1], line(-1), line(0)))

    loads[0].wait()
    tiles = lax.fori_loop(
        0, 8, lambda x, t: pack(t, x, lambda a, b, c: adj[0, a, b, c, x + 1, pl.ds(8, 8), :]), (zero, zero)
    )
    for t in (2, 1, 0):
        loads[1 + t].wait()

    def prepare(n, _):
        t, x = n // 8, n % 8
        rho, mx, my, mz = f_moments(lambda a, b, c: pops[t, 9 * a + 3 * b + c, x])
        flow[t, 0, x] = rho
        flow[t, 1, x] = mx / rho
        flow[t, 2, x] = my / rho
        flow[t, 3, x] = mz / rho
        return 0

    lax.fori_loop(0, STEPS * 8, prepare, 0)
    loads[4].wait()
    loads[5].wait()

    pl.semaphore_wait(barrier, count)
    start(0, tiles)

    for r in range(STEPS):
        t = STEPS - 1 - r
        last = r == STEPS - 1
        arrive(r)
        above, below = edge(r, -1), edge(r, 1)

        def step(x, tiles):
            p = [[[None] * 3 for _ in range(3)] for _ in range(3)]
            for a, b in PAIRS:
                spot = (3 * a + b) * 8 + x
                low, mid, high = (adj[r, a, b, c, x + a, pl.ds(7 + b, 8), :] for c in range(3))
                low = jnp.where(lane == 0, pltpu.roll(below, (128 - spot) & 127, 1), pltpu.roll(low, 1, 1))
                high = jnp.where(lane == 127, pltpu.roll(above, 127 - spot, 1), pltpu.roll(high, 127, 1))
                p[a][b] = [low, mid, high]
            p0, (px, py, pz), (pxx, pyy, pzz, pxy, pxz, pyz) = weighted_moments(p)
            rho, ux, uy, uz = (flow[t, k, x] for k in range(4))
            is_fluid = flu[x] == 1
            s = jnp.where(is_fluid, por[x], 1.0)
            usq = 1.5 * (ux * ux + uy * uy + uz * uz)
            qx = pxx * ux + pxy * uy + pxz * uz
            qy = pxy * ux + pyy * uy + pyz * uz
            qz = pxz * ux + pyz * uy + pzz * uz
            uq = 4.5 * (ux * qx + uy * qy + uz * qz)
            factor = (1.0 - s) * (1.6 / 216.0)
            base = factor * (p0 + (usq * p0 - uq))
            three = 3.0 * factor
            bx = three * (px - ux * p0 + 3.0 * qx)
            by = three * (py - uy * p0 + 3.0 * qy)
            bz = three * (pz - uz * p0 + 3.0 * qz)
            keep = -0.6 * (1.0 - s)

            total = None
            for a, b in PAIRS:
                for c in range(3):
                    i = 9 * a + 3 * b + c
                    term = p[a][b][c] * (pops[t, 26 - i, x] + 0.6 * pops[t, i, x])
                    total = term if total is None else total + term
            total = total - (1.6 / 216.0) * rho * (p0 - usq * p0 + 3.0 * (px * ux + py * uy + pz * uz) + uq)
            total = jnp.where(is_fluid, total, 0.0)
            acc[x] = total if r == 0 else acc[x] + total

            new = {}
            for a in range(3):
                ga = (base - bx, base, base + bx)[a]
                for b in range(3):
                    gb = (ga - by, ga, ga + by)[b]
                    for c in range(3):
                        g = (gb - bz, gb, gb + bz)[c]
                        value = keep * p[a][b][c] + (s * p[2 - a][2 - b][2 - c] + g)
                        new[a, b, c] = value
                        if last:
                            res[9 * a + 3 * b + c, x] = value
                        else:
                            adj[r + 1, a, b, c, x + 1, pl.ds(8, 8), :] = value
            if last:
                pltpu.make_async_copy(res.at[:, x], out.at[:, x], osem.at[x]).start()
                return tiles
            return pack(tiles, x, lambda a, b, c: new[a, b, c])

        tiles = lax.fori_loop(0, 8, step, (zero, zero))
        if not last:
            start(r + 1, tiles)

    done = pltpu.make_async_copy(acc, grad, osem.at[8])
    done.start()
    for r in range(STEPS):
        made = copies(r)
        for off in OFFSETS:
            pl.when(exists(off))(made[off].wait_send)
    for x in range(8):
        pltpu.make_async_copy(res.at[:, x], out.at[:, x], osem.at[x]).wait()
    done.wait()


def solution(mesh):
    sizes = tuple(mesh.shape[a] for a in AXES)
    f32 = jnp.float32
    call = pl.pallas_call(
        functools.partial(kernel, sizes),
        out_shape=(
            jax.ShapeDtypeStruct((27, 8, 8, 128), f32),
            jax.ShapeDtypeStruct((8, 8, 128), f32),
        ),
        in_specs=[pl.BlockSpec(memory_space=pl.ANY)] * 4,
        out_specs=[pl.BlockSpec(memory_space=pl.ANY)] * 2,
        scratch_shapes=[
            pltpu.VMEM((STEPS, 3, 3, 3, 10, 24, 128), f32),
            pltpu.VMEM((STEPS, 27, 8, 8, 128), f32),
            pltpu.VMEM((STEPS, 4, 8, 8, 128), f32),
            pltpu.VMEM((8, 8, 128), f32),
            pltpu.VMEM((8, 8, 128), jnp.int32),
            pltpu.VMEM((27, 8, 8, 128), f32),
            pltpu.VMEM((8, 8, 128), f32),
            pltpu.VMEM((STEPS, 2, 8, 128), f32),
            pltpu.VMEM((STEPS, 26, 8, 128), f32),
            pltpu.SemaphoreType.DMA((6,)),
            pltpu.SemaphoreType.DMA((9,)),
            pltpu.SemaphoreType.DMA((STEPS, 26)),
            pltpu.SemaphoreType.DMA((STEPS, 26)),
        ],
        compiler_params=pltpu.CompilerParams(
            collective_id=0, has_side_effects=True, vmem_limit_bytes=40 * 1024 * 1024
        ),
    )

    def local(saved, porosity, fluid, seed_adjoint):
        return call(saved, porosity, fluid, seed_adjoint.reshape(3, 3, 3, 8, 8, 128))

    return jax.shard_map(
        local,
        mesh=mesh,
        in_specs=(
            P(None, None, "gx", "gy", "gz"),
            P("gx", "gy", "gz"),
            P("gx", "gy", "gz"),
            P(None, "gx", "gy", "gz"),
        ),
        out_specs=(P(None, "gx", "gy", "gz"), P("gx", "gy", "gz")),
        check_vma=False,
    )
```

```python
import functools
import itertools

import jax
import jax.numpy as jnp
from jax import lax
from jax.experimental import pallas as pl
from jax.experimental.pallas import tpu as pltpu
from jax.sharding import PartitionSpec as P

STEPS = 3
AXES = ("gx", "gy", "gz")
OFFSETS = sorted(
    (o for o in itertools.product((-1, 0, 1), repeat=3) if any(o)),
    key=lambda o: (o[2] != 0, sum(map(abs, o)), o[0] != 0),
)
PAIRS = tuple(itertools.product(range(3), range(3)))


def f_moments(pops):
    s = [[pops(a, b, 0) + pops(a, b, 1) + pops(a, b, 2) for b in range(3)] for a in range(3)]
    dz = [sum(pops(a, b, 2) - pops(a, b, 0) for b in range(3)) for a in range(3)]
    sy = [s[a][0] + s[a][1] + s[a][2] for a in range(3)]
    dy = [s[a][2] - s[a][0] for a in range(3)]
    return (
        sy[0] + sy[1] + sy[2],
        sy[2] - sy[0],
        dy[0] + dy[1] + dy[2],
        dz[0] + dz[1] + dz[2],
    )


def even(v):
    side = v[0] + v[2]
    return 4.0 * v[1] + side, v[2] - v[0], side


def weighted_moments(p):
    z = [[even([p[a][b][c] for c in range(3)]) for b in range(3)] for a in range(3)]
    y = []
    for a in range(3):
        z0, z1, z2 = ([z[a][b][k] for b in range(3)] for k in range(3))
        y00, y10, y20 = even(z0)
        y01, y11, _ = even(z1)
        y02, _, _ = even(z2)
        y.append((y00, y10, y20, y01, y11, y02))
    p0, px, pxx = even([y[a][0] for a in range(3)])
    py, pxy, _ = even([y[a][1] for a in range(3)])
    pyy, _, _ = even([y[a][2] for a in range(3)])
    pz, pxz, _ = even([y[a][3] for a in range(3)])
    pyz, _, _ = even([y[a][4] for a in range(3)])
    pzz, _, _ = even([y[a][5] for a in range(3)])
    return p0, (px, py, pz), (pxx, pyy, pzz, pxy, pxz, pyz)


def kernel(
    sizes, saved, poro, fluid, seed, out, grad,
    adj, pops, flow, por, flu, ztile, zrecv,
    lsem, ssem, rsem,
):
    me = [lax.axis_index(a) for a in AXES]

    def exists(off):
        found = None
        for i, o in enumerate(off):
            if o:
                here = me[i] < sizes[i] - 1 if o > 0 else me[i] > 0
                found = here if found is None else jnp.logical_and(found, here)
        return found

    def device(off):
        return tuple(m + o for m, o in zip(me, off))

    def back(off):
        return tuple(-o for o in off)

    loads = [pltpu.make_async_copy(seed, adj.at[0, :, :, :, pl.ds(1, 8), pl.ds(8, 8), :], lsem.at[0])]
    loads += [pltpu.make_async_copy(saved.at[t], pops.at[t], lsem.at[1 + t]) for t in range(STEPS)]
    loads += [pltpu.make_async_copy(poro, por, lsem.at[4]), pltpu.make_async_copy(fluid, flu, lsem.at[5])]

    barrier = pltpu.get_barrier_semaphore()
    count = jnp.int32(0)
    for off in OFFSETS:
        there = exists(off)

        @pl.when(there)
        def _():
            pl.semaphore_signal(barrier, inc=1, device_id=device(off), device_id_type=pl.DeviceIdType.MESH)

        count = count + there.astype(jnp.int32)

    for i in (0, 3, 2, 1, 4, 5):
        loads[i].start()

    zero = jnp.zeros((8, 128), jnp.float32)
    for off in ((-1, 0, 0), (1, 0, 0)):

        @pl.when(jnp.logical_not(exists(off)))
        def _():
            part = 0 if off[0] < 0 else 9

            def clear(r, _):
                for b, c in PAIRS:
                    for tile in range(3):
                        adj[r, 1 + off[0], b, c, part, pl.ds(8 * tile, 8), :] = zero
                return 0

            lax.fori_loop(0, STEPS, clear, 0)

    for off in ((0, -1, 0), (0, 1, 0)):

        @pl.when(jnp.logical_not(exists(off)))
        def _():
            def clear(n, _):
                r, x = n // 10, n % 10
                for a, c in PAIRS:
                    row = 0 if off[1] < 0 else 16
                    adj[r, a, 1 + off[1], c, x, pl.ds(row, 8), :] = zero
                return 0

            lax.fori_loop(0, STEPS * 10, clear, 0)

    for k, off in enumerate(OFFSETS):
        if off[2]:

            @pl.when(jnp.logical_not(exists(back(off))))
            def _():
                for r in range(STEPS):
                    zrecv[r, k] = zero

    lane = lax.broadcasted_iota(jnp.int32, (8, 128), 1)
    row = lax.broadcasted_iota(jnp.int32, (8, 128), 0)
    group = lane >> 3
    inner = lane & 7
    ymod = jnp.where(group < 3, group, jnp.where(group < 6, group - 3, group - 6))
    xmask = {1: (group < 3) & (inner == 0), -1: (group >= 6) & (inner == 7)}
    ymask = {1: (ymod == 0) & (row == 0), -1: (ymod == 2) & (row == 7)}

    def copies(r):
        made = {}
        for k, (dx, dy, dz) in enumerate(OFFSETS):
            a, b = 1 - dx, 1 - dy
            xs, xd = (8, 0) if dx > 0 else (1, 9)
            ys, yd = (15, 7) if dy > 0 else (8, 16)
            if dz:
                src, dst = ztile.at[r, (1 - dz) // 2], zrecv.at[r, k]
            elif not dx:
                src = adj.at[r, :, b, :, pl.ds(1, 8), pl.ds(ys, 1), :]
                dst = adj.at[r, :, b, :, pl.ds(1, 8), pl.ds(yd, 1), :]
            elif not dy:
                src = adj.at[r, a, :, :, xs, pl.ds(8, 8), :]
                dst = adj.at[r, a, :, :, xd, pl.ds(8, 8), :]
            else:
                src = adj.at[r, a, b, :, xs, pl.ds(ys, 1), :]
                dst = adj.at[r, a, b, :, xd, pl.ds(yd, 1), :]
            off = (dx, dy, dz)
            made[off] = pltpu.make_async_remote_copy(
                src, dst, ssem.at[r, k], rsem.at[r, k],
                device_id=device(off), device_id_type=pl.DeviceIdType.MESH,
            )
        return made

    def pack(tiles, x, value):
        lower, upper = tiles
        for a, b in PAIRS:
            spot = (3 * a + b) * 8 + ((x + 1 - a) & 7)
            here = lane == spot
            upper = jnp.where(here, pltpu.roll(value(a, b, 0), spot + 1, 1), upper)
            lower = jnp.where(here, pltpu.roll(value(a, b, 2), spot, 1), lower)
        return lower, upper

    def shifted(tile):
        return jnp.where(ymod == 1, tile, jnp.where(ymod == 0, pltpu.roll(tile, 1, 0), pltpu.roll(tile, 7, 0)))

    def start(r, tiles):
        ztile[r, 1] = shifted(tiles[0])
        ztile[r, 0] = shifted(tiles[1])
        made = copies(r)
        for off in OFFSETS:
            pl.when(exists(off))(made[off].start)

    def arrive(r):
        made = copies(r)
        for off in OFFSETS:
            pl.when(exists(back(off)))(made[off].wait_recv)

    def edge(r, dz):
        def at(dx, dy):
            return zrecv[r, OFFSETS.index((dx, dy, dz))]

        def line(dx):
            return jnp.where(ymask[1], at(dx, 1), jnp.where(ymask[-1], at(dx, -1), at(dx, 0)))

        return jnp.where(xmask[1], line(1), jnp.where(xmask[-1], line(-1), line(0)))

    loads[0].wait()
    tiles = lax.fori_loop(
        0, 8, lambda x, t: pack(t, x, lambda a, b, c: adj[0, a, b, c, x + 1, pl.ds(8, 8), :]), (zero, zero)
    )
    for t in (2, 1, 0):
        loads[1 + t].wait()

    def prepare(n, _):
        t, x = n // 8, n % 8
        rho, mx, my, mz = f_moments(lambda a, b, c: pops[t, 9 * a + 3 * b + c, x])
        flow[t, 0, x] = rho
        flow[t, 1, x] = mx / rho
        flow[t, 2, x] = my / rho
        flow[t, 3, x] = mz / rho
        return 0

    lax.fori_loop(0, STEPS * 8, prepare, 0)
    loads[4].wait()
    loads[5].wait()

    pl.semaphore_wait(barrier, count)
    start(0, tiles)

    for r in range(STEPS):
        t = STEPS - 1 - r
        last = r == STEPS - 1
        arrive(r)
        above, below = edge(r, -1), edge(r, 1)

        def step(x, tiles):
            p = [[[None] * 3 for _ in range(3)] for _ in range(3)]
            for a, b in PAIRS:
                spot = (3 * a + b) * 8 + x
                low, mid, high = (adj[r, a, b, c, x + a, pl.ds(7 + b, 8), :] for c in range(3))
                low = jnp.where(lane == 0, pltpu.roll(below, (128 - spot) & 127, 1), pltpu.roll(low, 1, 1))
                high = jnp.where(lane == 127, pltpu.roll(above, 127 - spot, 1), pltpu.roll(high, 127, 1))
                p[a][b] = [low, mid, high]
            p0, (px, py, pz), (pxx, pyy, pzz, pxy, pxz, pyz) = weighted_moments(p)
            rho, ux, uy, uz = (flow[t, k, x] for k in range(4))
            is_fluid = flu[x] == 1
            s = jnp.where(is_fluid, por[x], 1.0)
            usq = 1.5 * (ux * ux + uy * uy + uz * uz)
            qx = pxx * ux + pxy * uy + pxz * uz
            qy = pxy * ux + pyy * uy + pyz * uz
            qz = pxz * ux + pyz * uy + pzz * uz
            uq = 4.5 * (ux * qx + uy * qy + uz * qz)
            factor = (1.0 - s) * (1.6 / 216.0)
            base = factor * (p0 + (usq * p0 - uq))
            three = 3.0 * factor
            bx = three * (px - ux * p0 + 3.0 * qx)
            by = three * (py - uy * p0 + 3.0 * qy)
            bz = three * (pz - uz * p0 + 3.0 * qz)
            keep = -0.6 * (1.0 - s)

            total = None
            for a, b in PAIRS:
                for c in range(3):
                    i = 9 * a + 3 * b + c
                    term = p[a][b][c] * (pops[t, 26 - i, x] + 0.6 * pops[t, i, x])
                    total = term if total is None else total + term
            total = total - (1.6 / 216.0) * rho * (p0 - usq * p0 + 3.0 * (px * ux + py * uy + pz * uz) + uq)
            total = jnp.where(is_fluid, total, 0.0)
            grad[x] = total if r == 0 else grad[x] + total

            new = {}
            for a in range(3):
                ga = (base - bx, base, base + bx)[a]
                for b in range(3):
                    gb = (ga - by, ga, ga + by)[b]
                    for c in range(3):
                        g = (gb - bz, gb, gb + bz)[c]
                        value = keep * p[a][b][c] + (s * p[2 - a][2 - b][2 - c] + g)
                        new[a, b, c] = value
                        if last:
                            out[9 * a + 3 * b + c, x] = value
                        else:
                            adj[r + 1, a, b, c, x + 1, pl.ds(8, 8), :] = value
            if last:
                return tiles
            return pack(tiles, x, lambda a, b, c: new[a, b, c])

        tiles = lax.fori_loop(0, 8, step, (zero, zero), unroll=8)
        if not last:
            start(r + 1, tiles)

    for r in range(STEPS):
        made = copies(r)
        for off in OFFSETS:
            pl.when(exists(off))(made[off].wait_send)


def solution(mesh):
    sizes = tuple(mesh.shape[a] for a in AXES)
    f32 = jnp.float32
    call = pl.pallas_call(
        functools.partial(kernel, sizes),
        out_shape=(
            pltpu.VMEM((27, 8, 8, 128), f32),
            pltpu.VMEM((8, 8, 128), f32),
        ),
        in_specs=[pl.BlockSpec(memory_space=pltpu.HBM)] * 4,
        out_specs=[pl.BlockSpec(memory_space=pltpu.VMEM)] * 2,
        scratch_shapes=[
            pltpu.VMEM((STEPS, 3, 3, 3, 10, 24, 128), f32),
            pltpu.VMEM((STEPS, 27, 8, 8, 128), f32),
            pltpu.VMEM((STEPS, 4, 8, 8, 128), f32),
            pltpu.VMEM((8, 8, 128), f32),
            pltpu.VMEM((8, 8, 128), jnp.int32),
            pltpu.VMEM((STEPS, 2, 8, 128), f32),
            pltpu.VMEM((STEPS, 26, 8, 128), f32),
            pltpu.SemaphoreType.DMA((6,)),
            pltpu.SemaphoreType.DMA((STEPS, 26)),
            pltpu.SemaphoreType.DMA((STEPS, 26)),
        ],
        compiler_params=pltpu.CompilerParams(
            collective_id=0, has_side_effects=True, vmem_limit_bytes=60 * 1024 * 1024
        ),
    )

    def local(saved, porosity, fluid, seed_adjoint):
        return call(saved, porosity, fluid, seed_adjoint.reshape(3, 3, 3, 8, 8, 128))

    return jax.shard_map(
        local,
        mesh=mesh,
        in_specs=(
            P(None, None, "gx", "gy", "gz"),
            P("gx", "gy", "gz"),
            P("gx", "gy", "gz"),
            P(None, "gx", "gy", "gz"),
        ),
        out_specs=(P(None, "gx", "gy", "gz"), P("gx", "gy", "gz")),
        check_vma=False,
    )
```

```python
import functools
import itertools

import jax
import jax.numpy as jnp
from jax import lax
from jax.experimental import pallas as pl
from jax.experimental.pallas import tpu as pltpu
from jax.sharding import PartitionSpec as P

STEPS = 3
AXES = ("gx", "gy", "gz")
OFFSETS = sorted(
    (o for o in itertools.product((-1, 0, 1), repeat=3) if any(o)),
    key=lambda o: (not o[1], -sum(map(abs, o))),
)
PAIRS = tuple(itertools.product(range(3), range(3)))


def f_moments(pops):
    s = [[pops(a, b, 0) + pops(a, b, 1) + pops(a, b, 2) for b in range(3)] for a in range(3)]
    dz = [sum(pops(a, b, 2) - pops(a, b, 0) for b in range(3)) for a in range(3)]
    sy = [s[a][0] + s[a][1] + s[a][2] for a in range(3)]
    dy = [s[a][2] - s[a][0] for a in range(3)]
    return (
        sy[0] + sy[1] + sy[2],
        sy[2] - sy[0],
        dy[0] + dy[1] + dy[2],
        dz[0] + dz[1] + dz[2],
    )


def even(v):
    side = v[0] + v[2]
    return 4.0 * v[1] + side, v[2] - v[0], side


def weighted_moments(p):
    z = [[even([p[a][b][c] for c in range(3)]) for b in range(3)] for a in range(3)]
    y = []
    for a in range(3):
        z0, z1, z2 = ([z[a][b][k] for b in range(3)] for k in range(3))
        y00, y10, y20 = even(z0)
        y01, y11, _ = even(z1)
        y02, _, _ = even(z2)
        y.append((y00, y10, y20, y01, y11, y02))
    p0, px, pxx = even([y[a][0] for a in range(3)])
    py, pxy, _ = even([y[a][1] for a in range(3)])
    pyy, _, _ = even([y[a][2] for a in range(3)])
    pz, pxz, _ = even([y[a][3] for a in range(3)])
    pyz, _, _ = even([y[a][4] for a in range(3)])
    pzz, _, _ = even([y[a][5] for a in range(3)])
    return p0, (px, py, pz), (pxx, pyy, pzz, pxy, pxz, pyz)


def positions():
    lane = lax.broadcasted_iota(jnp.int32, (8, 128), 1)
    row = lax.broadcasted_iota(jnp.int32, (8, 128), 0)
    group = lane >> 3
    ymod = jnp.where(group < 3, group, jnp.where(group < 6, group - 3, group - 6))
    return lane, row, group, ymod


def pull(adj, x, edges, lane):
    above, below = edges
    p = [[None] * 3 for _ in range(3)]
    for a, b in PAIRS:
        spot = (3 * a + b) * 8 + x
        low, mid, high = (adj[a, b, c, x + a, pl.ds(7 + b, 8), :] for c in range(3))
        low = jnp.where(lane == 0, pltpu.roll(below, (128 - spot) & 127, 1), pltpu.roll(low, 1, 1))
        high = jnp.where(lane == 127, pltpu.roll(above, 127 - spot, 1), pltpu.roll(high, 127, 1))
        p[a][b] = [low, mid, high]
    return p


def terms(p, flow, x):
    p0, first, (pxx, pyy, pzz, pxy, pxz, pyz) = weighted_moments(p)
    ux, uy, uz = (flow[k, x] for k in (1, 2, 3))
    usq = 1.5 * (ux * ux + uy * uy + uz * uz)
    qx = pxx * ux + pxy * uy + pxz * uz
    qy = pxy * ux + pyy * uy + pyz * uz
    qz = pxz * ux + pyz * uy + pzz * uz
    uq = 4.5 * (ux * qx + uy * qy + uz * qz)
    return p0, first, (ux, uy, uz), usq, (qx, qy, qz), uq


def new_adjoint(p, moments, s, store):
    p0, (px, py, pz), (ux, uy, uz), usq, (qx, qy, qz), uq = moments
    factor = (1.0 - s) * (1.6 / 216.0)
    base = factor * (p0 + (usq * p0 - uq))
    three = 3.0 * factor
    bx = three * (px - ux * p0 + 3.0 * qx)
    by = three * (py - uy * p0 + 3.0 * qy)
    bz = three * (pz - uz * p0 + 3.0 * qz)
    keep = -0.6 * (1.0 - s)
    for a in range(3):
        ga = (base - bx, base, base + bx)[a]
        for b in range(3):
            gb = (ga - by, ga, ga + by)[b]
            for c in range(3):
                g = (gb - bz, gb, gb + bz)[c]
                store(a, b, c, keep * p[a][b][c] + (s * p[2 - a][2 - b][2 - c] + g))


def porosity_term(p, moments, rho, pops, x):
    p0, (px, py, pz), (ux, uy, uz), usq, _, uq = moments
    total = None
    for a, b in PAIRS:
        for c in range(3):
            i = 9 * a + 3 * b + c
            term = p[a][b][c] * (pops[26 - i, x] + 0.6 * pops[i, x])
            total = term if total is None else total + term
    return total - (1.6 / 216.0) * rho * (p0 - usq * p0 + 3.0 * (px * ux + py * uy + pz * uz) + uq)


def last_kernel(adj, edges, pops, flow, por, flu, acc, out, grad, res, total, sem):
    lane = positions()[0]
    sides = edges[0], edges[1]
    for x in range(8):
        p = pull(adj, x, sides, lane)
        moments = terms(p, flow, x)
        is_fluid = flu[x] == 1

        def store(a, b, c, value):
            res[9 * a + 3 * b + c, x] = value

        new_adjoint(p, moments, jnp.where(is_fluid, por[x], 1.0), store)
        pltpu.make_async_copy(res.at[:, x], out.at[:, x], sem.at[x]).start()
        total[x] = acc[x] + jnp.where(is_fluid, porosity_term(p, moments, flow[0, x], pops, x), 0.0)
    done = pltpu.make_async_copy(total, grad, sem.at[8])
    done.start()
    for x in range(8):
        pltpu.make_async_copy(res.at[:, x], out.at[:, x], sem.at[x]).wait()
    done.wait()


def kernel(
    sizes, saved, poro, fluid, seed,
    adj2, edges, pops0, flow0, por, flu, acc,
    adj01, pops12, flow12, ztile, zrecv,
    lsem, ssem, rsem,
):
    adjs = (adj01.at[0], adj01.at[1], adj2)
    pops = (pops0, pops12.at[0], pops12.at[1])
    flow = (flow0, flow12.at[0], flow12.at[1])
    me = [lax.axis_index(a) for a in AXES]

    def exists(off):
        found = None
        for i, o in enumerate(off):
            if o:
                here = me[i] < sizes[i] - 1 if o > 0 else me[i] > 0
                found = here if found is None else jnp.logical_and(found, here)
        return found

    def device(off):
        return tuple(m + o for m, o in zip(me, off))

    def back(off):
        return tuple(-o for o in off)

    loads = [pltpu.make_async_copy(seed, adjs[0].at[:, :, :, pl.ds(1, 8), pl.ds(8, 8), :], lsem.at[0])]
    loads += [pltpu.make_async_copy(saved.at[t], pops[t], lsem.at[1 + t]) for t in range(STEPS)]
    loads += [pltpu.make_async_copy(poro, por, lsem.at[4]), pltpu.make_async_copy(fluid, flu, lsem.at[5])]

    barrier = pltpu.get_barrier_semaphore()
    count = jnp.int32(0)
    for off in OFFSETS:
        there = exists(off)

        @pl.when(there)
        def _():
            pl.semaphore_signal(barrier, inc=1, device_id=device(off), device_id_type=pl.DeviceIdType.MESH)

        count = count + there.astype(jnp.int32)

    for i in (0, 3, 2, 1, 4, 5):
        loads[i].start()

    zero = jnp.zeros((8, 128), jnp.float32)
    for off in ((-1, 0, 0), (1, 0, 0)):

        @pl.when(jnp.logical_not(exists(off)))
        def _():
            part = 0 if off[0] < 0 else 9

            for adj in adjs:
                for b, c in PAIRS:
                    for tile in range(3):
                        adj[1 + off[0], b, c, part, pl.ds(8 * tile, 8), :] = zero

    for off in ((0, -1, 0), (0, 1, 0)):

        @pl.when(jnp.logical_not(exists(off)))
        def _():
            def clear(x, _):
                for adj in adjs:
                    for a, c in PAIRS:
                        adj[a, 1 + off[1], c, x, pl.ds(0 if off[1] < 0 else 16, 8), :] = zero
                return 0

            lax.fori_loop(0, 10, clear, 0)

    for k, off in enumerate(OFFSETS):
        if off[2]:

            @pl.when(jnp.logical_not(exists(back(off))))
            def _():
                for r in range(STEPS):
                    zrecv[r, k] = zero

    lane, row, group, ymod = positions()
    inner = lane & 7
    xmask = {1: (group < 3) & (inner == 0), -1: (group >= 6) & (inner == 7)}
    ymask = {1: (ymod == 0) & (row == 0), -1: (ymod == 2) & (row == 7)}

    def copies(r):
        made = {}
        for k, (dx, dy, dz) in enumerate(OFFSETS):
            a, b = 1 - dx, 1 - dy
            xs, xd = (8, 0) if dx > 0 else (1, 9)
            ys, yd = (15, 7) if dy > 0 else (8, 16)
            if dz:
                rows = pl.ds(7 * b // 2, 1) if dy else pl.ds(0, 8)
                src, dst = ztile.at[r, (1 - dz) // 2, rows], zrecv.at[r, k, rows]
            elif not dx:
                src = adjs[r].at[:, b, :, pl.ds(1, 8), pl.ds(ys, 1), :]
                dst = adjs[r].at[:, b, :, pl.ds(1, 8), pl.ds(yd, 1), :]
            elif not dy:
                src = adjs[r].at[a, :, :, xs, pl.ds(8, 8), :]
                dst = adjs[r].at[a, :, :, xd, pl.ds(8, 8), :]
            else:
                src = adjs[r].at[a, b, :, xs, pl.ds(ys, 1), :]
                dst = adjs[r].at[a, b, :, xd, pl.ds(yd, 1), :]
            off = (dx, dy, dz)
            made[off] = pltpu.make_async_remote_copy(
                src, dst, ssem.at[r, k], rsem.at[r, k],
                device_id=device(off), device_id_type=pl.DeviceIdType.MESH,
            )
        return made

    def pack(tiles, x, value):
        lower, upper = tiles
        for a, b in PAIRS:
            spot = (3 * a + b) * 8 + ((x + 1 - a) & 7)
            here = lane == spot
            upper = jnp.where(here, pltpu.roll(value(a, b, 0), spot + 1, 1), upper)
            lower = jnp.where(here, pltpu.roll(value(a, b, 2), spot, 1), lower)
        return lower, upper

    def shifted(tile):
        return jnp.where(ymod == 1, tile, jnp.where(ymod == 0, pltpu.roll(tile, 1, 0), pltpu.roll(tile, 7, 0)))

    def start(r, tiles):
        ztile[r, 1] = shifted(tiles[0])
        ztile[r, 0] = shifted(tiles[1])
        made = copies(r)
        for off in OFFSETS:
            pl.when(exists(off))(made[off].start)

    def arrive(r):
        made = copies(r)
        for off in reversed(OFFSETS):
            pl.when(exists(back(off)))(made[off].wait_recv)

    def edge(r, dz):
        def at(dx, dy):
            return zrecv[r, OFFSETS.index((dx, dy, dz))]

        def line(dx):
            return jnp.where(ymask[1], at(dx, 1), jnp.where(ymask[-1], at(dx, -1), at(dx, 0)))

        return jnp.where(xmask[1], line(1), jnp.where(xmask[-1], line(-1), line(0)))

    loads[0].wait()
    tiles = lax.fori_loop(
        0, 8, lambda x, t: pack(t, x, lambda a, b, c: adjs[0][a, b, c, x + 1, pl.ds(8, 8), :]), (zero, zero)
    )
    for t in (2, 1, 0):
        loads[1 + t].wait()

    def prepare(x, _):
        for t in range(STEPS):
            rho, mx, my, mz = f_moments(lambda a, b, c: pops[t][9 * a + 3 * b + c, x])
            flow[t][0, x] = rho
            flow[t][1, x] = mx / rho
            flow[t][2, x] = my / rho
            flow[t][3, x] = mz / rho
        return 0

    lax.fori_loop(0, 8, prepare, 0)
    loads[4].wait()
    loads[5].wait()

    pl.semaphore_wait(barrier, count)
    start(0, tiles)

    for r in range(STEPS - 1):
        t = STEPS - 1 - r
        arrive(r)
        sides = edge(r, -1), edge(r, 1)

        def step(x, tiles):
            p = pull(adjs[r], x, sides, lane)
            new = {}

            def store(a, b, c, value):
                new[a, b, c] = value
                adjs[r + 1][a, b, c, x + 1, pl.ds(8, 8), :] = value

            new_adjoint(p, terms(p, flow[t], x), jnp.where(flu[x] == 1, por[x], 1.0), store)
            return pack(tiles, x, lambda a, b, c: new[a, b, c])

        start(r + 1, lax.fori_loop(0, 8, step, (zero, zero), unroll=8))

        def gradient(x, _):
            p = pull(adjs[r], x, sides, lane)
            term = porosity_term(p, terms(p, flow[t], x), flow[t][0, x], pops[t], x)
            term = jnp.where(flu[x] == 1, term, 0.0)
            acc[x] = term if r == 0 else acc[x] + term
            return 0

        lax.fori_loop(0, 8, gradient, 0)

    arrive(STEPS - 1)
    edges[0] = edge(STEPS - 1, -1)
    edges[1] = edge(STEPS - 1, 1)
    for r in range(STEPS):
        made = copies(r)
        for off in OFFSETS:
            pl.when(exists(off))(made[off].wait_send)


def solution(mesh):
    sizes = tuple(mesh.shape[a] for a in AXES)
    f32 = jnp.float32
    vmem, tiles = pl.BlockSpec(memory_space=pltpu.VMEM), (8, 8, 128)
    between = (
        pltpu.VMEM((3, 3, 3, 10, 24, 128), f32),
        pltpu.VMEM((2, 8, 128), f32),
        pltpu.VMEM((27, *tiles), f32),
        pltpu.VMEM((4, *tiles), f32),
        pltpu.VMEM(tiles, f32),
        pltpu.VMEM(tiles, jnp.int32),
        pltpu.VMEM(tiles, f32),
    )
    exchange = pl.pallas_call(
        functools.partial(kernel, sizes),
        out_shape=between,
        in_specs=[pl.BlockSpec(memory_space=pltpu.HBM)] * 4,
        out_specs=[vmem] * len(between),
        scratch_shapes=[
            pltpu.VMEM((2, 3, 3, 3, 10, 24, 128), f32),
            pltpu.VMEM((2, 27, *tiles), f32),
            pltpu.VMEM((2, 4, *tiles), f32),
            pltpu.VMEM((STEPS, 2, 8, 128), f32),
            pltpu.VMEM((STEPS, 26, 8, 128), f32),
            pltpu.SemaphoreType.DMA((6,)),
            pltpu.SemaphoreType.DMA((STEPS, 26)),
            pltpu.SemaphoreType.DMA((STEPS, 26)),
        ],
        compiler_params=pltpu.CompilerParams(
            collective_id=0, has_side_effects=True, vmem_limit_bytes=56 * 1024 * 1024
        ),
    )
    last = pl.pallas_call(
        last_kernel,
        out_shape=(jax.ShapeDtypeStruct((27, *tiles), f32), jax.ShapeDtypeStruct(tiles, f32)),
        in_specs=[vmem] * len(between),
        out_specs=[pl.BlockSpec(memory_space=pltpu.HBM)] * 2,
        scratch_shapes=[
            pltpu.VMEM((27, *tiles), f32),
            pltpu.VMEM(tiles, f32),
            pltpu.SemaphoreType.DMA((9,)),
        ],
        compiler_params=pltpu.CompilerParams(vmem_limit_bytes=48 * 1024 * 1024),
    )

    def local(saved, porosity, fluid, seed_adjoint):
        return last(*exchange(saved, porosity, fluid, seed_adjoint.reshape(3, 3, 3, 8, 8, 128)))

    return jax.shard_map(
        local,
        mesh=mesh,
        in_specs=(
            P(None, None, "gx", "gy", "gz"),
            P("gx", "gy", "gz"),
            P("gx", "gy", "gz"),
            P(None, "gx", "gy", "gz"),
        ),
        out_specs=(P(None, "gx", "gy", "gz"), P("gx", "gy", "gz")),
        check_vma=False,
    )
```

```python
import functools
import itertools

import jax
import jax.numpy as jnp
from jax import lax
from jax.experimental import pallas as pl
from jax.experimental.pallas import tpu as pltpu
from jax.sharding import PartitionSpec as P

STEPS = 3
AXES = ("gx", "gy", "gz")
OFFSETS = sorted(
    (o for o in itertools.product((-1, 0, 1), repeat=3) if any(o)),
    key=lambda o: (not o[1], -sum(map(abs, o))),
)
PAIRS = tuple(itertools.product(range(3), range(3)))


def f_moments(pops):
    s = [[pops(a, b, 0) + pops(a, b, 1) + pops(a, b, 2) for b in range(3)] for a in range(3)]
    dz = [sum(pops(a, b, 2) - pops(a, b, 0) for b in range(3)) for a in range(3)]
    sy = [s[a][0] + s[a][1] + s[a][2] for a in range(3)]
    dy = [s[a][2] - s[a][0] for a in range(3)]
    return (
        sy[0] + sy[1] + sy[2],
        sy[2] - sy[0],
        dy[0] + dy[1] + dy[2],
        dz[0] + dz[1] + dz[2],
    )


def even(v):
    side = v[0] + v[2]
    return 4.0 * v[1] + side, v[2] - v[0], side


def weighted_moments(p):
    z = [[even([p[a][b][c] for c in range(3)]) for b in range(3)] for a in range(3)]
    y = []
    for a in range(3):
        z0, z1, z2 = ([z[a][b][k] for b in range(3)] for k in range(3))
        y00, y10, y20 = even(z0)
        y01, y11, _ = even(z1)
        y02, _, _ = even(z2)
        y.append((y00, y10, y20, y01, y11, y02))
    p0, px, pxx = even([y[a][0] for a in range(3)])
    py, pxy, _ = even([y[a][1] for a in range(3)])
    pyy, _, _ = even([y[a][2] for a in range(3)])
    pz, pxz, _ = even([y[a][3] for a in range(3)])
    pyz, _, _ = even([y[a][4] for a in range(3)])
    pzz, _, _ = even([y[a][5] for a in range(3)])
    return p0, (px, py, pz), (pxx, pyy, pzz, pxy, pxz, pyz)


def positions():
    lane = lax.broadcasted_iota(jnp.int32, (8, 128), 1)
    row = lax.broadcasted_iota(jnp.int32, (8, 128), 0)
    group = lane >> 3
    ymod = jnp.where(group < 3, group, jnp.where(group < 6, group - 3, group - 6))
    return lane, row, group, ymod


def pull(read, shift, edges, lane):
    above, below = edges
    p = [[None] * 3 for _ in range(3)]
    for a, b in PAIRS:
        spot = (3 * a + b) * 8 + shift
        low, mid, high = (read(a, b, c) for c in range(3))
        low = jnp.where(lane == 0, pltpu.roll(below, (128 - spot) & 127, 1), pltpu.roll(low, 1, 1))
        high = jnp.where(lane == 127, pltpu.roll(above, 127 - spot, 1), pltpu.roll(high, 127, 1))
        p[a][b] = [low, mid, high]
    return p


def slice_of(adj, x):
    return lambda a, b, c: adj[a, b, c, x + a, pl.ds(7 + b, 8), :]


def terms(p, velocity):
    p0, first, (pxx, pyy, pzz, pxy, pxz, pyz) = weighted_moments(p)
    ux, uy, uz = velocity
    usq = 1.5 * (ux * ux + uy * uy + uz * uz)
    qx = pxx * ux + pxy * uy + pxz * uz
    qy = pxy * ux + pyy * uy + pyz * uz
    qz = pxz * ux + pyz * uy + pzz * uz
    uq = 4.5 * (ux * qx + uy * qy + uz * qz)
    return p0, first, (ux, uy, uz), usq, (qx, qy, qz), uq


def new_adjoint(p, moments, s, store, only=(0, 1, 2)):
    p0, (px, py, pz), (ux, uy, uz), usq, (qx, qy, qz), uq = moments
    factor = (1.0 - s) * (1.6 / 216.0)
    base = factor * (p0 + (usq * p0 - uq))
    three = 3.0 * factor
    bx = three * (px - ux * p0 + 3.0 * qx)
    by = three * (py - uy * p0 + 3.0 * qy)
    bz = three * (pz - uz * p0 + 3.0 * qz)
    keep = -0.6 * (1.0 - s)
    for a in range(3):
        ga = (base - bx, base, base + bx)[a]
        for b in only:
            gb = (ga - by, ga, ga + by)[b]
            for c in range(3):
                g = (gb - bz, gb, gb + bz)[c]
                store(a, b, c, keep * p[a][b][c] + (s * p[2 - a][2 - b][2 - c] + g))


def porosity_term(p, moments, rho, pops, x):
    p0, (px, py, pz), (ux, uy, uz), usq, _, uq = moments
    total = None
    for a, b in PAIRS:
        for c in range(3):
            i = 9 * a + 3 * b + c
            term = p[a][b][c] * (pops[26 - i, x] + 0.6 * pops[i, x])
            total = term if total is None else total + term
    return total - (1.6 / 216.0) * rho * (p0 - usq * p0 + 3.0 * (px * ux + py * uy + pz * uz) + uq)


def last_kernel(adj, edges, pops, flow, por, flu, acc, out, grad, res, total, sem):
    lane = positions()[0]
    sides = edges[0], edges[1]
    for x in range(8):
        p = pull(slice_of(adj, x), x, sides, lane)
        moments = terms(p, [flow[k, x] for k in (1, 2, 3)])
        is_fluid = flu[x] == 1

        def store(a, b, c, value):
            res[9 * a + 3 * b + c, x] = value

        new_adjoint(p, moments, jnp.where(is_fluid, por[x], 1.0), store)
        pltpu.make_async_copy(res.at[:, x], out.at[:, x], sem.at[x]).start()
        total[x] = acc[x] + jnp.where(is_fluid, porosity_term(p, moments, flow[0, x], pops, x), 0.0)
    done = pltpu.make_async_copy(total, grad, sem.at[8])
    done.start()
    for x in range(8):
        pltpu.make_async_copy(res.at[:, x], out.at[:, x], sem.at[x]).wait()
    done.wait()


def kernel(
    sizes, saved, poro, fluid, seed,
    adj2, edges, pops0, flow0, por, flu, acc,
    adj01, pops12, flow12, ztile, zrecv, plane, zrow,
    lsem, ssem, rsem,
):
    adjs = (adj01.at[0], adj01.at[1], adj2)
    pops = (pops0, pops12.at[0], pops12.at[1])
    flow = (flow0, flow12.at[0], flow12.at[1])
    me = [lax.axis_index(a) for a in AXES]

    def exists(off):
        found = None
        for i, o in enumerate(off):
            if o:
                here = me[i] < sizes[i] - 1 if o > 0 else me[i] > 0
                found = here if found is None else jnp.logical_and(found, here)
        return found

    def device(off):
        return tuple(m + o for m, o in zip(me, off))

    def back(off):
        return tuple(-o for o in off)

    loads = [pltpu.make_async_copy(seed, adjs[0].at[:, :, :, pl.ds(1, 8), pl.ds(8, 8), :], lsem.at[0])]
    loads += [pltpu.make_async_copy(saved.at[t], pops[t], lsem.at[1 + t]) for t in range(STEPS)]
    loads += [pltpu.make_async_copy(poro, por, lsem.at[4]), pltpu.make_async_copy(fluid, flu, lsem.at[5])]

    barrier = pltpu.get_barrier_semaphore()
    count = jnp.int32(0)
    for off in OFFSETS:
        there = exists(off)

        @pl.when(there)
        def _():
            pl.semaphore_signal(barrier, inc=1, device_id=device(off), device_id_type=pl.DeviceIdType.MESH)

        count = count + there.astype(jnp.int32)

    for i in (0, 3, 2, 1, 4, 5):
        loads[i].start()

    zero = jnp.zeros((8, 128), jnp.float32)
    for off in ((-1, 0, 0), (1, 0, 0)):

        @pl.when(jnp.logical_not(exists(off)))
        def _():
            part = 0 if off[0] < 0 else 9

            for adj in adjs:
                for b, c in PAIRS:
                    for tile in range(3):
                        adj[1 + off[0], b, c, part, pl.ds(8 * tile, 8), :] = zero

    for off in ((0, -1, 0), (0, 1, 0)):

        @pl.when(jnp.logical_not(exists(off)))
        def _():
            def clear(x, _):
                for adj in adjs:
                    for a, c in PAIRS:
                        adj[a, 1 + off[1], c, x, pl.ds(0 if off[1] < 0 else 16, 8), :] = zero
                return 0

            lax.fori_loop(0, 10, clear, 0)

    for k, off in enumerate(OFFSETS):
        if off[2]:

            @pl.when(jnp.logical_not(exists(back(off))))
            def _():
                for r in range(STEPS):
                    zrecv[r, k] = zero

    lane, row, group, ymod = positions()
    inner = lane & 7
    xmask = {1: (group < 3) & (inner == 0), -1: (group >= 6) & (inner == 7)}
    ymask = {1: (ymod == 0) & (row == 0), -1: (ymod == 2) & (row == 7)}

    def copies(r):
        made = {}
        for k, (dx, dy, dz) in enumerate(OFFSETS):
            a, b = 1 - dx, 1 - dy
            xs, xd = (8, 0) if dx > 0 else (1, 9)
            ys, yd = (15, 7) if dy > 0 else (8, 16)
            if dz:
                rows = pl.ds(7 * b // 2, 1) if dy else pl.ds(0, 8)
                src, dst = ztile.at[r, (1 - dz) // 2, rows], zrecv.at[r, k, rows]
                if dy and r:
                    src = zrow.at[r - 1, b // 2, (1 - dz) // 2, rows]
            elif not dx:
                src = adjs[r].at[:, b, :, pl.ds(1, 8), ys, :]
                dst = adjs[r].at[:, b, :, pl.ds(1, 8), yd, :]
                if r:
                    src = plane.at[r - 1, b // 2]
            elif not dy:
                src = adjs[r].at[a, :, :, xs, pl.ds(8, 8), :]
                dst = adjs[r].at[a, :, :, xd, pl.ds(8, 8), :]
            else:
                src = adjs[r].at[a, b, :, xs, pl.ds(ys, 1), :]
                dst = adjs[r].at[a, b, :, xd, pl.ds(yd, 1), :]
                if r:
                    src = plane.at[r - 1, b // 2, a, :, pl.ds(xs - 1, 1), :]
            off = (dx, dy, dz)
            made[off] = pltpu.make_async_remote_copy(
                src, dst, ssem.at[r, k], rsem.at[r, k],
                device_id=device(off), device_id_type=pl.DeviceIdType.MESH,
            )
        return made

    def pack(tiles, x, value):
        lower, upper = tiles
        for a, b in PAIRS:
            spot = (3 * a + b) * 8 + ((x + 1 - a) & 7)
            here = lane == spot
            upper = jnp.where(here, pltpu.roll(value(a, b, 0), spot + 1, 1), upper)
            lower = jnp.where(here, pltpu.roll(value(a, b, 2), spot, 1), lower)
        return lower, upper

    def shifted(tile):
        return jnp.where(ymod == 1, tile, jnp.where(ymod == 0, pltpu.roll(tile, 1, 0), pltpu.roll(tile, 7, 0)))

    def fill(r, tiles):
        ztile[r, 1] = shifted(tiles[0])
        ztile[r, 0] = shifted(tiles[1])

    def start(r, offsets):
        made = copies(r)
        for off in offsets:
            pl.when(exists(off))(made[off].start)

    far = [off for off in OFFSETS if off[1]]
    near = [off for off in OFFSETS if not off[1]]

    def along(tile, y):
        v = jnp.where(inner == row, jnp.broadcast_to(tile[y : y + 1], (8, 128)), 0.0)
        for n in (127, 126, 124):
            v = v + pltpu.roll(v, n, 1)
        return v

    def outer_plane(r, t, y, sides):
        flat = adjs[r].reshape(6480, 128)
        rates = flow[t].reshape(256, 128)
        there = pl.ds(y, 8, stride=8)
        p = pull(
            lambda a, b, c: flat[pl.ds(((9 * a + 3 * b + c) * 10 + a) * 24 + 7 + b + y, 8, stride=24), :],
            0, [along(side, y) for side in sides], lane,
        )
        s = jnp.where(flu.reshape(64, 128)[there, :] == 1, por.reshape(64, 128)[there, :], 1.0)
        b = 0 if y else 2
        new = {}

        def store(a, _, c, value):
            new[a, c] = value
            plane[r, b // 2, a, c] = value

        new_adjoint(p, terms(p, [rates[pl.ds(64 * k + y, 8, stride=8), :] for k in (1, 2, 3)]), s, store, (b,))
        for c, edge_lane in ((2, 0), (0, 127)):
            packed = zero
            for a in range(3):
                here = lane == (3 * a + b) * 8 + ((row + 1 - a) & 7)
                packed = jnp.where(here, jnp.broadcast_to(new[a, c][:, edge_lane : edge_lane + 1], (8, 128)), packed)
            for n in (4, 2, 1):
                packed = packed + pltpu.roll(packed, n, 0)
            zrow[r, b // 2, c // 2] = packed

    def arrive(r):
        made = copies(r)
        for off in reversed(OFFSETS):
            pl.when(exists(back(off)))(made[off].wait_recv)

    def leave(r):
        made = copies(r)
        for off in OFFSETS:
            pl.when(exists(off))(made[off].wait_send)

    def edge(r, dz):
        def at(dx, dy):
            return zrecv[r, OFFSETS.index((dx, dy, dz))]

        def line(dx):
            return jnp.where(ymask[1], at(dx, 1), jnp.where(ymask[-1], at(dx, -1), at(dx, 0)))

        return jnp.where(xmask[1], line(1), jnp.where(xmask[-1], line(-1), line(0)))

    loads[0].wait()
    tiles = lax.fori_loop(
        0, 8, lambda x, t: pack(t, x, lambda a, b, c: adjs[0][a, b, c, x + 1, pl.ds(8, 8), :]), (zero, zero)
    )
    for t in (2, 1, 0):
        loads[1 + t].wait()

    def prepare(x, _):
        for t in range(STEPS):
            rho, mx, my, mz = f_moments(lambda a, b, c: pops[t][9 * a + 3 * b + c, x])
            flow[t][0, x] = rho
            flow[t][1, x] = mx / rho
            flow[t][2, x] = my / rho
            flow[t][3, x] = mz / rho
        return 0

    lax.fori_loop(0, 8, prepare, 0)
    loads[4].wait()
    loads[5].wait()

    fill(0, tiles)
    pl.semaphore_wait(barrier, count)
    start(0, OFFSETS)

    for r in range(STEPS - 1):
        t = STEPS - 1 - r
        arrive(r)
        sides = edge(r, -1), edge(r, 1)

        outer_plane(r, t, 0, sides)
        outer_plane(r, t, 7, sides)
        start(r + 1, far)

        def step(x, tiles):
            p = pull(slice_of(adjs[r], x), x, sides, lane)
            new = {}

            def store(a, b, c, value):
                new[a, b, c] = value
                adjs[r + 1][a, b, c, x + 1, pl.ds(8, 8), :] = value

            new_adjoint(p, terms(p, [flow[t][k, x] for k in (1, 2, 3)]), jnp.where(flu[x] == 1, por[x], 1.0), store)
            return pack(tiles, x, lambda a, b, c: new[a, b, c])

        fill(r + 1, lax.fori_loop(0, 8, step, (zero, zero), unroll=8))
        start(r + 1, near)

        def gradient(x, _):
            p = pull(slice_of(adjs[r], x), x, sides, lane)
            term = porosity_term(p, terms(p, [flow[t][k, x] for k in (1, 2, 3)]), flow[t][0, x], pops[t], x)
            term = jnp.where(flu[x] == 1, term, 0.0)
            acc[x] = term if r == 0 else acc[x] + term
            return 0

        lax.fori_loop(0, 8, gradient, 0)
        leave(r)

    leave(STEPS - 1)
    arrive(STEPS - 1)
    edges[0] = edge(STEPS - 1, -1)
    edges[1] = edge(STEPS - 1, 1)


def solution(mesh):
    sizes = tuple(mesh.shape[a] for a in AXES)
    f32 = jnp.float32
    vmem, tiles = pl.BlockSpec(memory_space=pltpu.VMEM), (8, 8, 128)
    between = (
        pltpu.VMEM((3, 3, 3, 10, 24, 128), f32),
        pltpu.VMEM((2, 8, 128), f32),
        pltpu.VMEM((27, *tiles), f32),
        pltpu.VMEM((4, *tiles), f32),
        pltpu.VMEM(tiles, f32),
        pltpu.VMEM(tiles, jnp.int32),
        pltpu.VMEM(tiles, f32),
    )
    exchange = pl.pallas_call(
        functools.partial(kernel, sizes),
        out_shape=between,
        in_specs=[pl.BlockSpec(memory_space=pltpu.HBM)] * 4,
        out_specs=[vmem] * len(between),
        scratch_shapes=[
            pltpu.VMEM((2, 3, 3, 3, 10, 24, 128), f32),
            pltpu.VMEM((2, 27, *tiles), f32),
            pltpu.VMEM((2, 4, *tiles), f32),
            pltpu.VMEM((STEPS, 2, 8, 128), f32),
            pltpu.VMEM((STEPS, 26, 8, 128), f32),
            pltpu.VMEM((2, 2, 3, 3, 8, 128), f32),
            pltpu.VMEM((2, 2, 2, 8, 128), f32),
            pltpu.SemaphoreType.DMA((6,)),
            pltpu.SemaphoreType.DMA((STEPS, 26)),
            pltpu.SemaphoreType.DMA((STEPS, 26)),
        ],
        compiler_params=pltpu.CompilerParams(
            collective_id=0, has_side_effects=True, vmem_limit_bytes=56 * 1024 * 1024
        ),
    )
    last = pl.pallas_call(
        last_kernel,
        out_shape=(jax.ShapeDtypeStruct((27, *tiles), f32), jax.ShapeDtypeStruct(tiles, f32)),
        in_specs=[vmem] * len(between),
        out_specs=[pl.BlockSpec(memory_space=pltpu.HBM)] * 2,
        scratch_shapes=[
            pltpu.VMEM((27, *tiles), f32),
            pltpu.VMEM(tiles, f32),
            pltpu.SemaphoreType.DMA((9,)),
        ],
        compiler_params=pltpu.CompilerParams(vmem_limit_bytes=48 * 1024 * 1024),
    )

    def local(saved, porosity, fluid, seed_adjoint):
        return last(*exchange(saved, porosity, fluid, seed_adjoint.reshape(3, 3, 3, 8, 8, 128)))

    return jax.shard_map(
        local,
        mesh=mesh,
        in_specs=(
            P(None, None, "gx", "gy", "gz"),
            P("gx", "gy", "gz"),
            P("gx", "gy", "gz"),
            P(None, "gx", "gy", "gz"),
        ),
        out_specs=(P(None, "gx", "gy", "gz"), P("gx", "gy", "gz")),
        check_vma=False,
    )
```

```python
import functools
import itertools

import jax
import jax.numpy as jnp
from jax import lax
from jax.experimental import pallas as pl
from jax.experimental.pallas import tpu as pltpu
from jax.sharding import PartitionSpec as P

STEPS = 3
AXES = ("gx", "gy", "gz")
OFFSETS = sorted(
    (o for o in itertools.product((-1, 0, 1), repeat=3) if any(o)),
    key=lambda o: (not o[1], bool(o[0] or o[2]), not o[2], bool(o[0])),
)
PAIRS = tuple(itertools.product(range(3), range(3)))


def f_moments(pops):
    s = [[pops(a, b, 0) + pops(a, b, 1) + pops(a, b, 2) for b in range(3)] for a in range(3)]
    dz = [sum(pops(a, b, 2) - pops(a, b, 0) for b in range(3)) for a in range(3)]
    sy = [s[a][0] + s[a][1] + s[a][2] for a in range(3)]
    dy = [s[a][2] - s[a][0] for a in range(3)]
    return (
        sy[0] + sy[1] + sy[2],
        sy[2] - sy[0],
        dy[0] + dy[1] + dy[2],
        dz[0] + dz[1] + dz[2],
    )


def even(v):
    side = v[0] + v[2]
    return 4.0 * v[1] + side, v[2] - v[0], side


def weighted_moments(p):
    z = [[even([p[a][b][c] for c in range(3)]) for b in range(3)] for a in range(3)]
    y = []
    for a in range(3):
        z0, z1, z2 = ([z[a][b][k] for b in range(3)] for k in range(3))
        y00, y10, y20 = even(z0)
        y01, y11, _ = even(z1)
        y02, _, _ = even(z2)
        y.append((y00, y10, y20, y01, y11, y02))
    p0, px, pxx = even([y[a][0] for a in range(3)])
    py, pxy, _ = even([y[a][1] for a in range(3)])
    pyy, _, _ = even([y[a][2] for a in range(3)])
    pz, pxz, _ = even([y[a][3] for a in range(3)])
    pyz, _, _ = even([y[a][4] for a in range(3)])
    pzz, _, _ = even([y[a][5] for a in range(3)])
    return p0, (px, py, pz), (pxx, pyy, pzz, pxy, pxz, pyz)


def positions():
    lane = lax.broadcasted_iota(jnp.int32, (8, 128), 1)
    row = lax.broadcasted_iota(jnp.int32, (8, 128), 0)
    group = lane >> 3
    ymod = jnp.where(group < 3, group, jnp.where(group < 6, group - 3, group - 6))
    return lane, row, group, ymod


def pull(read, shift, edges, lane):
    above, below = edges
    p = [[None] * 3 for _ in range(3)]
    for a, b in PAIRS:
        spot = (3 * a + b) * 8 + shift
        low, mid, high = (read(a, b, c) for c in range(3))
        if isinstance(below, list):
            lowest, highest = below[3 * a + b], above[3 * a + b]
        else:
            lowest, highest = pltpu.roll(below, (128 - spot) & 127, 1), pltpu.roll(above, 127 - spot, 1)
        low = jnp.where(lane == 0, lowest, pltpu.roll(low, 1, 1))
        high = jnp.where(lane == 127, highest, pltpu.roll(high, 127, 1))
        p[a][b] = [low, mid, high]
    return p


def slice_of(adj, x):
    return lambda a, b, c: adj[a, b, c, x + a, pl.ds(7 + b, 8), :]


def terms(p, velocity):
    p0, first, (pxx, pyy, pzz, pxy, pxz, pyz) = weighted_moments(p)
    ux, uy, uz = velocity
    usq = 1.5 * (ux * ux + uy * uy + uz * uz)
    qx = pxx * ux + pxy * uy + pxz * uz
    qy = pxy * ux + pyy * uy + pyz * uz
    qz = pxz * ux + pyz * uy + pzz * uz
    uq = 4.5 * (ux * qx + uy * qy + uz * qz)
    return p0, first, (ux, uy, uz), usq, (qx, qy, qz), uq


def new_adjoint(p, moments, s, store, only=(0, 1, 2)):
    p0, (px, py, pz), (ux, uy, uz), usq, (qx, qy, qz), uq = moments
    factor = (1.0 - s) * (1.6 / 216.0)
    base = factor * (p0 + (usq * p0 - uq))
    three = 3.0 * factor
    bx = three * (px - ux * p0 + 3.0 * qx)
    by = three * (py - uy * p0 + 3.0 * qy)
    bz = three * (pz - uz * p0 + 3.0 * qz)
    keep = -0.6 * (1.0 - s)
    for a in range(3):
        ga = (base - bx, base, base + bx)[a]
        for b in only:
            gb = (ga - by, ga, ga + by)[b]
            for c in range(3):
                g = (gb - bz, gb, gb + bz)[c]
                store(a, b, c, keep * p[a][b][c] + (s * p[2 - a][2 - b][2 - c] + g))


def porosity_term(p, moments, rho, pops, x):
    p0, (px, py, pz), (ux, uy, uz), usq, _, uq = moments
    total = None
    for a, b in PAIRS:
        for c in range(3):
            i = 9 * a + 3 * b + c
            term = p[a][b][c] * (pops[26 - i, x] + 0.6 * pops[i, x])
            total = term if total is None else total + term
    return total - (1.6 / 216.0) * rho * (p0 - usq * p0 + 3.0 * (px * ux + py * uy + pz * uz) + uq)


def last_kernel(adj, edges, pops, flow, por, flu, acc, out, grad, res, total, sem):
    lane = positions()[0]
    sides = edges[0], edges[1]
    for x in range(8):
        p = pull(slice_of(adj, x), x, sides, lane)
        moments = terms(p, [flow[k, x] for k in (1, 2, 3)])
        is_fluid = flu[x] == 1

        def store(a, b, c, value):
            res[9 * a + 3 * b + c, x] = value

        new_adjoint(p, moments, jnp.where(is_fluid, por[x], 1.0), store)
        pltpu.make_async_copy(res.at[:, x], out.at[:, x], sem.at[x]).start()
        total[x] = acc[x] + jnp.where(is_fluid, porosity_term(p, moments, flow[0, x], pops, x), 0.0)
    done = pltpu.make_async_copy(total, grad, sem.at[8])
    done.start()
    for x in range(8):
        pltpu.make_async_copy(res.at[:, x], out.at[:, x], sem.at[x]).wait()
    done.wait()


def kernel(
    sizes, saved, poro, fluid, seed,
    adj2, edges, pops0, flow0, por, flu, acc,
    adj01, pops12, flow12, ztile, zrecv, plane, zrow,
    lsem, ssem, rsem,
):
    adjs = (adj01.at[0], adj01.at[1], adj2)
    pops = (pops0, pops12.at[0], pops12.at[1])
    flow = (flow0, flow12.at[0], flow12.at[1])
    me = [lax.axis_index(a) for a in AXES]

    def exists(off):
        found = None
        for i, o in enumerate(off):
            if o:
                here = me[i] < sizes[i] - 1 if o > 0 else me[i] > 0
                found = here if found is None else jnp.logical_and(found, here)
        return found

    def device(off):
        return tuple(m + o for m, o in zip(me, off))

    def back(off):
        return tuple(-o for o in off)

    loads = [pltpu.make_async_copy(seed, adjs[0].at[:, :, :, pl.ds(1, 8), pl.ds(8, 8), :], lsem.at[0])]
    loads += [pltpu.make_async_copy(saved.at[t], pops[t], lsem.at[1 + t]) for t in range(STEPS)]
    loads += [pltpu.make_async_copy(poro, por, lsem.at[4]), pltpu.make_async_copy(fluid, flu, lsem.at[5])]

    barrier = pltpu.get_barrier_semaphore()
    count = jnp.int32(0)
    for off in OFFSETS:
        there = exists(off)

        @pl.when(there)
        def _():
            pl.semaphore_signal(barrier, inc=1, device_id=device(off), device_id_type=pl.DeviceIdType.MESH)

        count = count + there.astype(jnp.int32)

    for i in (0, 3, 2, 1, 4, 5):
        loads[i].start()

    zero = jnp.zeros((8, 128), jnp.float32)
    for off in ((-1, 0, 0), (1, 0, 0)):

        @pl.when(jnp.logical_not(exists(off)))
        def _():
            part = 0 if off[0] < 0 else 9

            for adj in adjs:
                for b, c in PAIRS:
                    for tile in range(3):
                        adj[1 + off[0], b, c, part, pl.ds(8 * tile, 8), :] = zero

    for off in ((0, -1, 0), (0, 1, 0)):

        @pl.when(jnp.logical_not(exists(off)))
        def _():
            def clear(x, _):
                for adj in adjs:
                    for a, c in PAIRS:
                        adj[a, 1 + off[1], c, x, pl.ds(0 if off[1] < 0 else 16, 8), :] = zero
                return 0

            lax.fori_loop(0, 10, clear, 0)

    for k, off in enumerate(OFFSETS):
        if off[2]:

            @pl.when(jnp.logical_not(exists(back(off))))
            def _():
                for r in range(STEPS):
                    zrecv[r, k] = zero

    lane, row, group, ymod = positions()
    inner = lane & 7
    xmask = {1: (group < 3) & (inner == 0), -1: (group >= 6) & (inner == 7)}
    ymask = {1: (ymod == 0) & (row == 0), -1: (ymod == 2) & (row == 7)}

    def copies(r):
        made = {}
        for k, (dx, dy, dz) in enumerate(OFFSETS):
            a, b = 1 - dx, 1 - dy
            xs, xd = (8, 0) if dx > 0 else (1, 9)
            ys, yd = (15, 7) if dy > 0 else (8, 16)
            if dz:
                rows = pl.ds(7 * b // 2, 1) if dy else pl.ds(0, 8)
                src, dst = ztile.at[r, (1 - dz) // 2, rows], zrecv.at[r, k, rows]
                if dy and r:
                    src = zrow.at[r - 1, b // 2, (1 - dz) // 2, rows]
            elif not dx:
                src = adjs[r].at[:, b, :, pl.ds(1, 8), ys, :]
                dst = adjs[r].at[:, b, :, pl.ds(1, 8), yd, :]
                if r:
                    src = plane.at[r - 1, b // 2]
            elif not dy:
                src = adjs[r].at[a, :, :, xs, pl.ds(8, 8), :]
                dst = adjs[r].at[a, :, :, xd, pl.ds(8, 8), :]
            else:
                src = adjs[r].at[a, b, :, xs, pl.ds(ys, 1), :]
                dst = adjs[r].at[a, b, :, xd, pl.ds(yd, 1), :]
                if r:
                    src = plane.at[r - 1, b // 2, a, :, pl.ds(xs - 1, 1), :]
            off = (dx, dy, dz)
            made[off] = pltpu.make_async_remote_copy(
                src, dst, ssem.at[r, k], rsem.at[r, k],
                device_id=device(off), device_id_type=pl.DeviceIdType.MESH,
            )
        return made

    def pack(tiles, x, value):
        lower, upper = tiles
        for a, b in PAIRS:
            spot = (3 * a + b) * 8 + ((x + 1 - a) & 7)
            here = lane == spot
            upper = jnp.where(here, pltpu.roll(value(a, b, 0), spot + 1, 1), upper)
            lower = jnp.where(here, pltpu.roll(value(a, b, 2), spot, 1), lower)
        return lower, upper

    def shifted(tile):
        return jnp.where(ymod == 1, tile, jnp.where(ymod == 0, pltpu.roll(tile, 1, 0), pltpu.roll(tile, 7, 0)))

    def fill(r, tiles):
        ztile[r, 1] = shifted(tiles[0])
        ztile[r, 0] = shifted(tiles[1])

    def start(r, offsets):
        made = copies(r)
        for off in offsets:
            pl.when(exists(off))(made[off].start)

    far = [off for off in OFFSETS if off[1]]
    near = [off for off in OFFSETS if not off[1]]

    def along(tile, y):
        v = jnp.where(inner == row, jnp.broadcast_to(tile[y : y + 1], (8, 128)), 0.0)
        return [jnp.sum(jnp.where(group == k, v, 0.0), axis=1, keepdims=True) for k in range(9)]

    def outer_plane(r, t, y, sides):
        flat = adjs[r].reshape(6480, 128)
        rates = flow[t].reshape(256, 128)
        there = pl.ds(y, 8, stride=8)
        p = pull(
            lambda a, b, c: flat[pl.ds(((9 * a + 3 * b + c) * 10 + a) * 24 + 7 + b + y, 8, stride=24), :],
            0, [along(side, y) for side in sides], lane,
        )
        s = jnp.where(flu.reshape(64, 128)[there, :] == 1, por.reshape(64, 128)[there, :], 1.0)
        b = 0 if y else 2
        new = {}

        def store(a, _, c, value):
            new[a, c] = value
            plane[r, b // 2, a, c] = value

        new_adjoint(p, terms(p, [rates[pl.ds(64 * k + y, 8, stride=8), :] for k in (1, 2, 3)]), s, store, (b,))
        for c, edge_lane in ((2, 0), (0, 127)):
            packed = zero
            for a in range(3):
                here = lane == (3 * a + b) * 8 + ((row + 1 - a) & 7)
                packed = jnp.where(here, jnp.broadcast_to(new[a, c][:, edge_lane : edge_lane + 1], (8, 128)), packed)
            for n in (4, 2, 1):
                packed = packed + pltpu.roll(packed, n, 0)
            zrow[r, b // 2, c // 2] = packed

    def arrive(r):
        made = copies(r)
        for off in reversed(OFFSETS):
            pl.when(exists(back(off)))(made[off].wait_recv)

    def leave(r):
        made = copies(r)
        for off in OFFSETS:
            pl.when(exists(off))(made[off].wait_send)

    def edge(r, dz):
        def at(dx, dy):
            return zrecv[r, OFFSETS.index((dx, dy, dz))]

        def line(dx):
            return jnp.where(ymask[1], at(dx, 1), jnp.where(ymask[-1], at(dx, -1), at(dx, 0)))

        return jnp.where(xmask[1], line(1), jnp.where(xmask[-1], line(-1), line(0)))

    loads[0].wait()
    tiles = lax.fori_loop(
        0, 8, lambda x, t: pack(t, x, lambda a, b, c: adjs[0][a, b, c, x + 1, pl.ds(8, 8), :]), (zero, zero)
    )
    for t in (2, 1, 0):
        loads[1 + t].wait()

    def prepare(x, _):
        for t in range(STEPS):
            rho, mx, my, mz = f_moments(lambda a, b, c: pops[t][9 * a + 3 * b + c, x])
            flow[t][0, x] = rho
            flow[t][1, x] = mx / rho
            flow[t][2, x] = my / rho
            flow[t][3, x] = mz / rho
        return 0

    lax.fori_loop(0, 8, prepare, 0)
    loads[4].wait()
    loads[5].wait()

    fill(0, tiles)
    pl.semaphore_wait(barrier, count)
    start(0, OFFSETS)

    for r in range(STEPS - 1):
        t = STEPS - 1 - r
        arrive(r)
        sides = edge(r, -1), edge(r, 1)

        outer_plane(r, t, 0, sides)
        outer_plane(r, t, 7, sides)
        start(r + 1, far)

        def step(x, tiles):
            p = pull(slice_of(adjs[r], x), x, sides, lane)
            new = {}

            def store(a, b, c, value):
                new[a, b, c] = value
                adjs[r + 1][a, b, c, x + 1, pl.ds(8, 8), :] = value

            new_adjoint(p, terms(p, [flow[t][k, x] for k in (1, 2, 3)]), jnp.where(flu[x] == 1, por[x], 1.0), store)
            return pack(tiles, x, lambda a, b, c: new[a, b, c])

        fill(r + 1, lax.fori_loop(0, 8, step, (zero, zero), unroll=8))
        start(r + 1, near)

        def gradient(x, _):
            p = pull(slice_of(adjs[r], x), x, sides, lane)
            term = porosity_term(p, terms(p, [flow[t][k, x] for k in (1, 2, 3)]), flow[t][0, x], pops[t], x)
            term = jnp.where(flu[x] == 1, term, 0.0)
            acc[x] = term if r == 0 else acc[x] + term
            return 0

        lax.fori_loop(0, 8, gradient, 0)
        leave(r)

    leave(STEPS - 1)
    arrive(STEPS - 1)
    edges[0] = edge(STEPS - 1, -1)
    edges[1] = edge(STEPS - 1, 1)


def solution(mesh):
    sizes = tuple(mesh.shape[a] for a in AXES)
    f32 = jnp.float32
    vmem, tiles = pl.BlockSpec(memory_space=pltpu.VMEM), (8, 8, 128)
    between = (
        pltpu.VMEM((3, 3, 3, 10, 24, 128), f32),
        pltpu.VMEM((2, 8, 128), f32),
        pltpu.VMEM((27, *tiles), f32),
        pltpu.VMEM((4, *tiles), f32),
        pltpu.VMEM(tiles, f32),
        pltpu.VMEM(tiles, jnp.int32),
        pltpu.VMEM(tiles, f32),
    )
    exchange = pl.pallas_call(
        functools.partial(kernel, sizes),
        out_shape=between,
        in_specs=[pl.BlockSpec(memory_space=pltpu.HBM)] * 4,
        out_specs=[vmem] * len(between),
        scratch_shapes=[
            pltpu.VMEM((2, 3, 3, 3, 10, 24, 128), f32),
            pltpu.VMEM((2, 27, *tiles), f32),
            pltpu.VMEM((2, 4, *tiles), f32),
            pltpu.VMEM((STEPS, 2, 8, 128), f32),
            pltpu.VMEM((STEPS, 26, 8, 128), f32),
            pltpu.VMEM((2, 2, 3, 3, 8, 128), f32),
            pltpu.VMEM((2, 2, 2, 8, 128), f32),
            pltpu.SemaphoreType.DMA((6,)),
            pltpu.SemaphoreType.DMA((STEPS, 26)),
            pltpu.SemaphoreType.DMA((STEPS, 26)),
        ],
        compiler_params=pltpu.CompilerParams(
            collective_id=0, has_side_effects=True, vmem_limit_bytes=56 * 1024 * 1024
        ),
    )
    last = pl.pallas_call(
        last_kernel,
        out_shape=(jax.ShapeDtypeStruct((27, *tiles), f32), jax.ShapeDtypeStruct(tiles, f32)),
        in_specs=[vmem] * len(between),
        out_specs=[pl.BlockSpec(memory_space=pltpu.HBM)] * 2,
        scratch_shapes=[
            pltpu.VMEM((27, *tiles), f32),
            pltpu.VMEM(tiles, f32),
            pltpu.SemaphoreType.DMA((9,)),
        ],
        compiler_params=pltpu.CompilerParams(vmem_limit_bytes=48 * 1024 * 1024),
    )

    def local(saved, porosity, fluid, seed_adjoint):
        return last(*exchange(saved, porosity, fluid, seed_adjoint.reshape(3, 3, 3, 8, 8, 128)))

    return jax.shard_map(
        local,
        mesh=mesh,
        in_specs=(
            P(None, None, "gx", "gy", "gz"),
            P("gx", "gy", "gz"),
            P("gx", "gy", "gz"),
            P(None, "gx", "gy", "gz"),
        ),
        out_specs=(P(None, "gx", "gy", "gz"), P("gx", "gy", "gz")),
        check_vma=False,
    )
```

```python
import functools
import itertools

import jax
import jax.numpy as jnp
from jax import lax
from jax.experimental import pallas as pl
from jax.experimental.pallas import tpu as pltpu
from jax.sharding import PartitionSpec as P

STEPS = 3
AXES = ("gx", "gy", "gz")
OFFSETS = sorted(
    (o for o in itertools.product((-1, 0, 1), repeat=3) if any(o)),
    key=lambda o: (not o[1], bool(o[0] or o[2]), not o[2], bool(o[0])),
)
PAIRS = tuple(itertools.product(range(3), range(3)))


def f_moments(pops):
    s = [[pops(a, b, 0) + pops(a, b, 1) + pops(a, b, 2) for b in range(3)] for a in range(3)]
    dz = [sum(pops(a, b, 2) - pops(a, b, 0) for b in range(3)) for a in range(3)]
    sy = [s[a][0] + s[a][1] + s[a][2] for a in range(3)]
    dy = [s[a][2] - s[a][0] for a in range(3)]
    return (
        sy[0] + sy[1] + sy[2],
        sy[2] - sy[0],
        dy[0] + dy[1] + dy[2],
        dz[0] + dz[1] + dz[2],
    )


def even(v):
    side = v[0] + v[2]
    return 4.0 * v[1] + side, v[2] - v[0], side


def weighted_moments(p):
    z = [[even([p[a][b][c] for c in range(3)]) for b in range(3)] for a in range(3)]
    y = []
    for a in range(3):
        z0, z1, z2 = ([z[a][b][k] for b in range(3)] for k in range(3))
        y00, y10, y20 = even(z0)
        y01, y11, _ = even(z1)
        y02, _, _ = even(z2)
        y.append((y00, y10, y20, y01, y11, y02))
    p0, px, pxx = even([y[a][0] for a in range(3)])
    py, pxy, _ = even([y[a][1] for a in range(3)])
    pyy, _, _ = even([y[a][2] for a in range(3)])
    pz, pxz, _ = even([y[a][3] for a in range(3)])
    pyz, _, _ = even([y[a][4] for a in range(3)])
    pzz, _, _ = even([y[a][5] for a in range(3)])
    return p0, (px, py, pz), (pxx, pyy, pzz, pxy, pxz, pyz)


def positions():
    lane = lax.broadcasted_iota(jnp.int32, (8, 128), 1)
    row = lax.broadcasted_iota(jnp.int32, (8, 128), 0)
    group = lane >> 3
    ymod = jnp.where(group < 3, group, jnp.where(group < 6, group - 3, group - 6))
    return lane, row, group, ymod


def pull(read, shift, edges, lane):
    above, below = edges
    p = [[None] * 3 for _ in range(3)]
    for a, b in PAIRS:
        spot = (3 * a + b) * 8 + shift
        low, mid, high = (read(a, b, c) for c in range(3))
        if isinstance(below, list):
            lowest, highest = below[3 * a + b], above[3 * a + b]
        else:
            lowest, highest = pltpu.roll(below, (128 - spot) & 127, 1), pltpu.roll(above, 127 - spot, 1)
        low = jnp.where(lane == 0, lowest, pltpu.roll(low, 1, 1))
        high = jnp.where(lane == 127, highest, pltpu.roll(high, 127, 1))
        p[a][b] = [low, mid, high]
    return p


def slice_of(adj, x):
    return lambda a, b, c: adj[a, b, c, x + a, pl.ds(7 + b, 8), :]


def terms(p, velocity):
    p0, first, (pxx, pyy, pzz, pxy, pxz, pyz) = weighted_moments(p)
    ux, uy, uz = velocity
    usq = 1.5 * (ux * ux + uy * uy + uz * uz)
    qx = pxx * ux + pxy * uy + pxz * uz
    qy = pxy * ux + pyy * uy + pyz * uz
    qz = pxz * ux + pyz * uy + pzz * uz
    uq = 4.5 * (ux * qx + uy * qy + uz * qz)
    return p0, first, (ux, uy, uz), usq, (qx, qy, qz), uq


def new_adjoint(p, moments, s, store, only=(0, 1, 2)):
    p0, (px, py, pz), (ux, uy, uz), usq, (qx, qy, qz), uq = moments
    factor = (1.0 - s) * (1.6 / 216.0)
    base = factor * (p0 + (usq * p0 - uq))
    three = 3.0 * factor
    bx = three * (px - ux * p0 + 3.0 * qx)
    by = three * (py - uy * p0 + 3.0 * qy)
    bz = three * (pz - uz * p0 + 3.0 * qz)
    keep = -0.6 * (1.0 - s)
    for a in range(3):
        ga = (base - bx, base, base + bx)[a]
        for b in only:
            gb = (ga - by, ga, ga + by)[b]
            for c in range(3):
                g = (gb - bz, gb, gb + bz)[c]
                store(a, b, c, keep * p[a][b][c] + (s * p[2 - a][2 - b][2 - c] + g))


def porosity_term(p, moments, rho, pops, x):
    p0, (px, py, pz), (ux, uy, uz), usq, _, uq = moments
    total = None
    for a, b in PAIRS:
        for c in range(3):
            i = 9 * a + 3 * b + c
            term = p[a][b][c] * (pops[26 - i, x] + 0.6 * pops[i, x])
            total = term if total is None else total + term
    return total - (1.6 / 216.0) * rho * (p0 - usq * p0 + 3.0 * (px * ux + py * uy + pz * uz) + uq)


def last_kernel(adj, edges, pops, flow, por, flu, acc, out, grad, res, total, sem):
    lane = positions()[0]
    sides = edges[0], edges[1]
    for x in range(8):
        p = pull(slice_of(adj, x), x, sides, lane)
        moments = terms(p, [flow[k, x] for k in (1, 2, 3)])
        is_fluid = flu[x] == 1

        def store(a, b, c, value):
            res[9 * a + 3 * b + c, x] = value

        new_adjoint(p, moments, jnp.where(is_fluid, por[x], 1.0), store)
        pltpu.make_async_copy(res.at[:, x], out.at[:, x], sem.at[x]).start()
        total[x] = acc[x] + jnp.where(is_fluid, porosity_term(p, moments, flow[0, x], pops, x), 0.0)
    done = pltpu.make_async_copy(total, grad, sem.at[8])
    done.start()
    for x in range(8):
        pltpu.make_async_copy(res.at[:, x], out.at[:, x], sem.at[x]).wait()
    done.wait()


def kernel(
    sizes, saved, poro, fluid, seed,
    adj2, edges, pops0, flow0, por, flu, acc,
    adj01, pops12, flow12, ztile, zrecv, plane, zrow,
    lsem, ssem, rsem,
):
    adjs = (adj01.at[0], adj01.at[1], adj2)
    pops = (pops0, pops12.at[0], pops12.at[1])
    flow = (flow0, flow12.at[0], flow12.at[1])
    me = [lax.axis_index(a) for a in AXES]

    def exists(off):
        found = None
        for i, o in enumerate(off):
            if o:
                here = me[i] < sizes[i] - 1 if o > 0 else me[i] > 0
                found = here if found is None else jnp.logical_and(found, here)
        return found

    def device(off):
        return tuple(m + o for m, o in zip(me, off))

    def back(off):
        return tuple(-o for o in off)

    loads = [pltpu.make_async_copy(seed, adjs[0].at[:, :, :, pl.ds(1, 8), pl.ds(8, 8), :], lsem.at[0])]
    loads += [pltpu.make_async_copy(saved.at[t], pops[t], lsem.at[1 + t]) for t in range(STEPS)]
    loads += [pltpu.make_async_copy(poro, por, lsem.at[4]), pltpu.make_async_copy(fluid, flu, lsem.at[5])]

    barrier = pltpu.get_barrier_semaphore()
    count = jnp.int32(0)
    for off in OFFSETS:
        there = exists(off)

        @pl.when(there)
        def _():
            pl.semaphore_signal(barrier, inc=1, device_id=device(off), device_id_type=pl.DeviceIdType.MESH)

        count = count + there.astype(jnp.int32)

    for i in (0, 3, 2, 1, 4, 5):
        loads[i].start()

    zero = jnp.zeros((8, 128), jnp.float32)
    lane, row, group, ymod = positions()
    inner = lane & 7
    xmask = {1: (group < 3) & (inner == 0), -1: (group >= 6) & (inner == 7)}
    ymask = {1: (ymod == 0) & (row == 0), -1: (ymod == 2) & (row == 7)}

    def copies(r):
        made = {}
        for k, (dx, dy, dz) in enumerate(OFFSETS):
            a, b = 1 - dx, 1 - dy
            xs, xd = (8, 0) if dx > 0 else (1, 9)
            ys, yd = (15, 7) if dy > 0 else (8, 16)
            if dz:
                rows = pl.ds(7 * b // 2, 1) if dy else pl.ds(0, 8)
                src, dst = ztile.at[r, (1 - dz) // 2, rows], zrecv.at[r, k, rows]
                if dy and r:
                    src = zrow.at[r - 1, b // 2, (1 - dz) // 2, rows]
            elif not dx:
                src = adjs[r].at[:, b, :, pl.ds(1, 8), ys, :]
                dst = adjs[r].at[:, b, :, pl.ds(1, 8), yd, :]
                if r:
                    src = plane.at[r - 1, b // 2]
            elif not dy:
                src = adjs[r].at[a, :, :, xs, pl.ds(8, 8), :]
                dst = adjs[r].at[a, :, :, xd, pl.ds(8, 8), :]
            else:
                src = adjs[r].at[a, b, :, xs, pl.ds(ys, 1), :]
                dst = adjs[r].at[a, b, :, xd, pl.ds(yd, 1), :]
                if r:
                    src = plane.at[r - 1, b // 2, a, :, pl.ds(xs - 1, 1), :]
            off = (dx, dy, dz)
            made[off] = pltpu.make_async_remote_copy(
                src, dst, ssem.at[r, k], rsem.at[r, k],
                device_id=device(off), device_id_type=pl.DeviceIdType.MESH,
            )
        return made

    def pack(tiles, x, value):
        lower, upper = tiles
        for a, b in PAIRS:
            spot = (3 * a + b) * 8 + ((x + 1 - a) & 7)
            here = lane == spot
            upper = jnp.where(here, pltpu.roll(value(a, b, 0), spot + 1, 1), upper)
            lower = jnp.where(here, pltpu.roll(value(a, b, 2), spot, 1), lower)
        return lower, upper

    def shifted(tile):
        return jnp.where(ymod == 1, tile, jnp.where(ymod == 0, pltpu.roll(tile, 1, 0), pltpu.roll(tile, 7, 0)))

    def fill(r, tiles):
        ztile[r, 1] = shifted(tiles[0])
        ztile[r, 0] = shifted(tiles[1])

    def start(r, offsets):
        made = copies(r)
        for off in offsets:
            pl.when(exists(off))(made[off].start)

    far = [off for off in OFFSETS if off[1]]
    near = [off for off in OFFSETS if not off[1]]

    def along(tile, y):
        v = jnp.where(inner == row, jnp.broadcast_to(tile[y : y + 1], (8, 128)), 0.0)
        return [jnp.sum(jnp.where(group == k, v, 0.0), axis=1, keepdims=True) for k in range(9)]

    def outer_plane(r, t, y, sides):
        flat = adjs[r].reshape(6480, 128)
        rates = flow[t].reshape(256, 128)
        there = pl.ds(y, 8, stride=8)
        p = pull(
            lambda a, b, c: flat[pl.ds(((9 * a + 3 * b + c) * 10 + a) * 24 + 7 + b + y, 8, stride=24), :],
            0, [along(side, y) for side in sides], lane,
        )
        s = jnp.where(flu.reshape(64, 128)[there, :] == 1, por.reshape(64, 128)[there, :], 1.0)
        b = 0 if y else 2
        new = {}

        def store(a, _, c, value):
            new[a, c] = value
            plane[r, b // 2, a, c] = value

        new_adjoint(p, terms(p, [rates[pl.ds(64 * k + y, 8, stride=8), :] for k in (1, 2, 3)]), s, store, (b,))
        for c, edge_lane in ((2, 0), (0, 127)):
            packed = zero
            for a in range(3):
                here = lane == (3 * a + b) * 8 + ((row + 1 - a) & 7)
                packed = jnp.where(here, jnp.broadcast_to(new[a, c][:, edge_lane : edge_lane + 1], (8, 128)), packed)
            for n in (4, 2, 1):
                packed = packed + pltpu.roll(packed, n, 0)
            zrow[r, b // 2, c // 2] = packed

    def arrive(r):
        made = copies(r)
        for off in reversed(OFFSETS):
            pl.when(exists(back(off)))(made[off].wait_recv)

    def leave(r):
        made = copies(r)
        for off in OFFSETS:
            pl.when(exists(off))(made[off].wait_send)

    def edge(r, dz):
        def at(dx, dy):
            return zrecv[r, OFFSETS.index((dx, dy, dz))]

        def line(dx):
            return jnp.where(ymask[1], at(dx, 1), jnp.where(ymask[-1], at(dx, -1), at(dx, 0)))

        return jnp.where(xmask[1], line(1), jnp.where(xmask[-1], line(-1), line(0)))

    loads[0].wait()
    tiles = lax.fori_loop(
        0, 8, lambda x, t: pack(t, x, lambda a, b, c: adjs[0][a, b, c, x + 1, pl.ds(8, 8), :]), (zero, zero),
        unroll=8,
    )
    fill(0, tiles)
    pl.semaphore_wait(barrier, count)
    start(0, OFFSETS)

    for off in ((-1, 0, 0), (1, 0, 0)):

        @pl.when(jnp.logical_not(exists(off)))
        def _():
            part = 0 if off[0] < 0 else 9

            for adj in adjs:
                for b, c in PAIRS:
                    for tile in range(3):
                        adj[1 + off[0], b, c, part, pl.ds(8 * tile, 8), :] = zero

    for off in ((0, -1, 0), (0, 1, 0)):

        @pl.when(jnp.logical_not(exists(off)))
        def _():
            def clear(x, _):
                for adj in adjs:
                    for a, c in PAIRS:
                        adj[a, 1 + off[1], c, x, pl.ds(0 if off[1] < 0 else 16, 8), :] = zero
                return 0

            lax.fori_loop(0, 10, clear, 0)

    for k, off in enumerate(OFFSETS):
        if off[2]:

            @pl.when(jnp.logical_not(exists(back(off))))
            def _():
                for r in range(STEPS):
                    zrecv[r, k] = zero

    for t in (2, 1, 0):
        loads[1 + t].wait()

    def prepare(x, _):
        for t in range(STEPS):
            rho, mx, my, mz = f_moments(lambda a, b, c: pops[t][9 * a + 3 * b + c, x])
            flow[t][0, x] = rho
            flow[t][1, x] = mx / rho
            flow[t][2, x] = my / rho
            flow[t][3, x] = mz / rho
        return 0

    lax.fori_loop(0, 8, prepare, 0)
    loads[4].wait()
    loads[5].wait()

    for r in range(STEPS - 1):
        t = STEPS - 1 - r
        arrive(r)
        sides = edge(r, -1), edge(r, 1)

        outer_plane(r, t, 0, sides)
        outer_plane(r, t, 7, sides)
        start(r + 1, far)

        def step(x, tiles):
            p = pull(slice_of(adjs[r], x), x, sides, lane)
            new = {}

            def store(a, b, c, value):
                new[a, b, c] = value
                adjs[r + 1][a, b, c, x + 1, pl.ds(8, 8), :] = value

            new_adjoint(p, terms(p, [flow[t][k, x] for k in (1, 2, 3)]), jnp.where(flu[x] == 1, por[x], 1.0), store)
            return pack(tiles, x, lambda a, b, c: new[a, b, c])

        fill(r + 1, lax.fori_loop(0, 8, step, (zero, zero), unroll=8))
        start(r + 1, near)

        def gradient(x, _):
            p = pull(slice_of(adjs[r], x), x, sides, lane)
            term = porosity_term(p, terms(p, [flow[t][k, x] for k in (1, 2, 3)]), flow[t][0, x], pops[t], x)
            term = jnp.where(flu[x] == 1, term, 0.0)
            acc[x] = term if r == 0 else acc[x] + term
            return 0

        lax.fori_loop(0, 8, gradient, 0)
        leave(r)

    leave(STEPS - 1)
    arrive(STEPS - 1)
    edges[0] = edge(STEPS - 1, -1)
    edges[1] = edge(STEPS - 1, 1)


def solution(mesh):
    sizes = tuple(mesh.shape[a] for a in AXES)
    f32 = jnp.float32
    vmem, tiles = pl.BlockSpec(memory_space=pltpu.VMEM), (8, 8, 128)
    between = (
        pltpu.VMEM((3, 3, 3, 10, 24, 128), f32),
        pltpu.VMEM((2, 8, 128), f32),
        pltpu.VMEM((27, *tiles), f32),
        pltpu.VMEM((4, *tiles), f32),
        pltpu.VMEM(tiles, f32),
        pltpu.VMEM(tiles, jnp.int32),
        pltpu.VMEM(tiles, f32),
    )
    exchange = pl.pallas_call(
        functools.partial(kernel, sizes),
        out_shape=between,
        in_specs=[pl.BlockSpec(memory_space=pltpu.HBM)] * 4,
        out_specs=[vmem] * len(between),
        scratch_shapes=[
            pltpu.VMEM((2, 3, 3, 3, 10, 24, 128), f32),
            pltpu.VMEM((2, 27, *tiles), f32),
            pltpu.VMEM((2, 4, *tiles), f32),
            pltpu.VMEM((STEPS, 2, 8, 128), f32),
            pltpu.VMEM((STEPS, 26, 8, 128), f32),
            pltpu.VMEM((2, 2, 3, 3, 8, 128), f32),
            pltpu.VMEM((2, 2, 2, 8, 128), f32),
            pltpu.SemaphoreType.DMA((6,)),
            pltpu.SemaphoreType.DMA((STEPS, 26)),
            pltpu.SemaphoreType.DMA((STEPS, 26)),
        ],
        compiler_params=pltpu.CompilerParams(
            collective_id=0, has_side_effects=True, vmem_limit_bytes=56 * 1024 * 1024
        ),
    )
    last = pl.pallas_call(
        last_kernel,
        out_shape=(jax.ShapeDtypeStruct((27, *tiles), f32), jax.ShapeDtypeStruct(tiles, f32)),
        in_specs=[vmem] * len(between),
        out_specs=[pl.BlockSpec(memory_space=pltpu.HBM)] * 2,
        scratch_shapes=[
            pltpu.VMEM((27, *tiles), f32),
            pltpu.VMEM(tiles, f32),
            pltpu.SemaphoreType.DMA((9,)),
        ],
        compiler_params=pltpu.CompilerParams(vmem_limit_bytes=48 * 1024 * 1024),
    )

    def local(saved, porosity, fluid, seed_adjoint):
        return last(*exchange(saved, porosity, fluid, seed_adjoint.reshape(3, 3, 3, 8, 8, 128)))

    return jax.shard_map(
        local,
        mesh=mesh,
        in_specs=(
            P(None, None, "gx", "gy", "gz"),
            P("gx", "gy", "gz"),
            P("gx", "gy", "gz"),
            P(None, "gx", "gy", "gz"),
        ),
        out_specs=(P(None, "gx", "gy", "gz"), P("gx", "gy", "gz")),
        check_vma=False,
    )
```

```python
import functools
import itertools

import jax
import jax.numpy as jnp
from jax import lax
from jax.experimental import pallas as pl
from jax.experimental.pallas import tpu as pltpu
from jax.sharding import PartitionSpec as P

STEPS = 3
AXES = ("gx", "gy", "gz")
OFFSETS = sorted(
    (o for o in itertools.product((-1, 0, 1), repeat=3) if any(o)),
    key=lambda o: (not o[1], bool(o[0] or o[2]), not o[2], bool(o[0])),
)
PAIRS = tuple(itertools.product(range(3), range(3)))


def f_moments(pops):
    s = [[pops(a, b, 0) + pops(a, b, 1) + pops(a, b, 2) for b in range(3)] for a in range(3)]
    dz = [sum(pops(a, b, 2) - pops(a, b, 0) for b in range(3)) for a in range(3)]
    sy = [s[a][0] + s[a][1] + s[a][2] for a in range(3)]
    dy = [s[a][2] - s[a][0] for a in range(3)]
    return (
        sy[0] + sy[1] + sy[2],
        sy[2] - sy[0],
        dy[0] + dy[1] + dy[2],
        dz[0] + dz[1] + dz[2],
    )


def even(v):
    side = v[0] + v[2]
    return 4.0 * v[1] + side, v[2] - v[0], side


def weighted_moments(p):
    z = [[even([p[a][b][c] for c in range(3)]) for b in range(3)] for a in range(3)]
    y = []
    for a in range(3):
        z0, z1, z2 = ([z[a][b][k] for b in range(3)] for k in range(3))
        y00, y10, y20 = even(z0)
        y01, y11, _ = even(z1)
        y02, _, _ = even(z2)
        y.append((y00, y10, y20, y01, y11, y02))
    p0, px, pxx = even([y[a][0] for a in range(3)])
    py, pxy, _ = even([y[a][1] for a in range(3)])
    pyy, _, _ = even([y[a][2] for a in range(3)])
    pz, pxz, _ = even([y[a][3] for a in range(3)])
    pyz, _, _ = even([y[a][4] for a in range(3)])
    pzz, _, _ = even([y[a][5] for a in range(3)])
    return p0, (px, py, pz), (pxx, pyy, pzz, pxy, pxz, pyz)


def positions():
    lane = lax.broadcasted_iota(jnp.int32, (8, 128), 1)
    row = lax.broadcasted_iota(jnp.int32, (8, 128), 0)
    group = lane >> 3
    ymod = jnp.where(group < 3, group, jnp.where(group < 6, group - 3, group - 6))
    return lane, row, group, ymod


def pull(read, shift, edges, lane):
    above, below = edges
    p = [[None] * 3 for _ in range(3)]
    for a, b in PAIRS:
        spot = (3 * a + b) * 8 + shift
        low, mid, high = (read(a, b, c) for c in range(3))
        if isinstance(below, list):
            lowest, highest = below[3 * a + b], above[3 * a + b]
        else:
            lowest, highest = pltpu.roll(below, (128 - spot) & 127, 1), pltpu.roll(above, 127 - spot, 1)
        low = jnp.where(lane == 0, lowest, pltpu.roll(low, 1, 1))
        high = jnp.where(lane == 127, highest, pltpu.roll(high, 127, 1))
        p[a][b] = [low, mid, high]
    return p


def slice_of(adj, x):
    return lambda a, b, c: adj[a, b, c, x + a, pl.ds(7 + b, 8), :]


def terms(p, velocity):
    p0, first, (pxx, pyy, pzz, pxy, pxz, pyz) = weighted_moments(p)
    ux, uy, uz = velocity
    usq = 1.5 * (ux * ux + uy * uy + uz * uz)
    qx = pxx * ux + pxy * uy + pxz * uz
    qy = pxy * ux + pyy * uy + pyz * uz
    qz = pxz * ux + pyz * uy + pzz * uz
    uq = 4.5 * (ux * qx + uy * qy + uz * qz)
    return p0, first, (ux, uy, uz), usq, (qx, qy, qz), uq


def new_adjoint(p, moments, s, store, only=(0, 1, 2)):
    p0, (px, py, pz), (ux, uy, uz), usq, (qx, qy, qz), uq = moments
    factor = (1.0 - s) * (1.6 / 216.0)
    base = factor * (p0 + (usq * p0 - uq))
    three = 3.0 * factor
    bx = three * (px - ux * p0 + 3.0 * qx)
    by = three * (py - uy * p0 + 3.0 * qy)
    bz = three * (pz - uz * p0 + 3.0 * qz)
    keep = -0.6 * (1.0 - s)
    for a in range(3):
        ga = (base - bx, base, base + bx)[a]
        for b in only:
            gb = (ga - by, ga, ga + by)[b]
            for c in range(3):
                g = (gb - bz, gb, gb + bz)[c]
                store(a, b, c, keep * p[a][b][c] + (s * p[2 - a][2 - b][2 - c] + g))


def porosity_term(p, moments, rho, pops, x):
    p0, (px, py, pz), (ux, uy, uz), usq, _, uq = moments
    total = None
    for a, b in PAIRS:
        for c in range(3):
            i = 9 * a + 3 * b + c
            term = p[a][b][c] * (pops[26 - i, x] + 0.6 * pops[i, x])
            total = term if total is None else total + term
    return total - (1.6 / 216.0) * rho * (p0 - usq * p0 + 3.0 * (px * ux + py * uy + pz * uz) + uq)


def last_kernel(adj, edges, pops, flow, por, flu, acc, out, grad, res, total, sem):
    lane = positions()[0]
    sides = edges[0], edges[1]
    for x in range(8):
        p = pull(slice_of(adj, x), x, sides, lane)
        moments = terms(p, [flow[k, x] for k in (1, 2, 3)])
        is_fluid = flu[x] == 1

        def store(a, b, c, value):
            res[9 * a + 3 * b + c, x] = value

        new_adjoint(p, moments, jnp.where(is_fluid, por[x], 1.0), store)
        pltpu.make_async_copy(res.at[:, x], out.at[:, x], sem.at[x]).start()
        total[x] = acc[x] + jnp.where(is_fluid, porosity_term(p, moments, flow[0, x], pops, x), 0.0)
    done = pltpu.make_async_copy(total, grad, sem.at[8])
    done.start()
    for x in range(8):
        pltpu.make_async_copy(res.at[:, x], out.at[:, x], sem.at[x]).wait()
    done.wait()


def kernel(
    sizes, saved, poro, fluid, seed,
    adj2, edges, pops0, flow0, por, flu, acc,
    adj01, pops12, flow12, ztile, zrecv, plane, zrow,
    lsem, ssem, rsem,
):
    adjs = (adj01.at[0], adj01.at[1], adj2)
    pops = (pops0, pops12.at[0], pops12.at[1])
    flow = (flow0, flow12.at[0], flow12.at[1])
    me = [lax.axis_index(a) for a in AXES]

    def exists(off):
        found = None
        for i, o in enumerate(off):
            if o:
                here = me[i] < sizes[i] - 1 if o > 0 else me[i] > 0
                found = here if found is None else jnp.logical_and(found, here)
        return found

    def device(off):
        return tuple(m + o for m, o in zip(me, off))

    def back(off):
        return tuple(-o for o in off)

    loads = [pltpu.make_async_copy(seed, adjs[0].at[:, :, :, pl.ds(1, 8), pl.ds(8, 8), :], lsem.at[0])]
    loads += [pltpu.make_async_copy(saved.at[t], pops[t], lsem.at[1 + t]) for t in range(STEPS)]
    loads += [pltpu.make_async_copy(poro, por, lsem.at[4]), pltpu.make_async_copy(fluid, flu, lsem.at[5])]

    barrier = pltpu.get_barrier_semaphore()
    count = jnp.int32(0)
    for off in OFFSETS:
        there = exists(off)

        @pl.when(there)
        def _():
            pl.semaphore_signal(barrier, inc=1, device_id=device(off), device_id_type=pl.DeviceIdType.MESH)

        count = count + there.astype(jnp.int32)

    for i in (0, 3, 2, 1, 4, 5):
        loads[i].start()

    zero = jnp.zeros((8, 128), jnp.float32)
    lane, row, group, ymod = positions()
    inner = lane & 7
    xmask = {1: (group < 3) & (inner == 0), -1: (group >= 6) & (inner == 7)}
    ymask = {1: (ymod == 0) & (row == 0), -1: (ymod == 2) & (row == 7)}

    def copies(r):
        made = {}
        for k, (dx, dy, dz) in enumerate(OFFSETS):
            a, b = 1 - dx, 1 - dy
            xs, xd = (8, 0) if dx > 0 else (1, 9)
            ys, yd = (15, 7) if dy > 0 else (8, 16)
            if dz:
                rows = pl.ds(7 * b // 2, 1) if dy else pl.ds(0, 8)
                src, dst = ztile.at[r, (1 - dz) // 2, rows], zrecv.at[r, k, rows]
                if dy and r:
                    src = zrow.at[r - 1, b // 2, (1 - dz) // 2, rows]
            elif not dx:
                src = adjs[r].at[:, b, :, pl.ds(1, 8), ys, :]
                dst = adjs[r].at[:, b, :, pl.ds(1, 8), yd, :]
                if r:
                    src = plane.at[r - 1, b // 2]
            elif not dy:
                src = adjs[r].at[a, :, :, xs, pl.ds(8, 8), :]
                dst = adjs[r].at[a, :, :, xd, pl.ds(8, 8), :]
            else:
                src = adjs[r].at[a, b, :, xs, pl.ds(ys, 1), :]
                dst = adjs[r].at[a, b, :, xd, pl.ds(yd, 1), :]
                if r:
                    src = plane.at[r - 1, b // 2, a, :, pl.ds(xs - 1, 1), :]
            off = (dx, dy, dz)
            made[off] = pltpu.make_async_remote_copy(
                src, dst, ssem.at[r, k], rsem.at[r, k],
                device_id=device(off), device_id_type=pl.DeviceIdType.MESH,
            )
        return made

    def pack(tiles, x, value):
        lower, upper = tiles
        for a, b in PAIRS:
            spot = (3 * a + b) * 8 + ((x + 1 - a) & 7)
            here = lane == spot
            upper = jnp.where(here, pltpu.roll(value(a, b, 0), spot + 1, 1), upper)
            lower = jnp.where(here, pltpu.roll(value(a, b, 2), spot, 1), lower)
        return lower, upper

    def shifted(tile):
        return jnp.where(ymod == 1, tile, jnp.where(ymod == 0, pltpu.roll(tile, 1, 0), pltpu.roll(tile, 7, 0)))

    def fill(r, tiles):
        ztile[r, 1] = shifted(tiles[0])
        ztile[r, 0] = shifted(tiles[1])

    def start(r, offsets):
        made = copies(r)
        for off in offsets:
            pl.when(exists(off))(made[off].start)

    far = [off for off in OFFSETS if off[1]]
    near = [off for off in OFFSETS if not off[1]]

    def along(tile, y):
        v = jnp.where(inner == row, jnp.broadcast_to(tile[y : y + 1], (8, 128)), 0.0)
        return [jnp.sum(jnp.where(group == k, v, 0.0), axis=1, keepdims=True) for k in range(9)]

    def outer_planes(r, t, sides):
        flat = adjs[r].reshape(6480, 128)
        rates = flow[t].reshape(256, 128)
        given, made = [], []
        for y in (0, 7):
            there = pl.ds(y, 8, stride=8)
            p = pull(
                lambda a, b, c: flat[pl.ds(((9 * a + 3 * b + c) * 10 + a) * 24 + 7 + b + y, 8, stride=24), :],
                0, [along(side, y) for side in sides], lane,
            )
            s = jnp.where(flu.reshape(64, 128)[there, :] == 1, por.reshape(64, 128)[there, :], 1.0)
            given.append((p, [rates[pl.ds(64 * k + y, 8, stride=8), :] for k in (1, 2, 3)], s))
        for (p, velocity, s), b in zip(given, (2, 0)):
            new = {}
            new_adjoint(p, terms(p, velocity), s, lambda a, _, c, value: new.update({(a, c): value}), (b,))
            rows = []
            for c, edge_lane in ((2, 0), (0, 127)):
                packed = zero
                for a in range(3):
                    here = lane == (3 * a + b) * 8 + ((row + 1 - a) & 7)
                    side = jnp.broadcast_to(new[a, c][:, edge_lane : edge_lane + 1], (8, 128))
                    packed = jnp.where(here, side, packed)
                for n in (4, 2, 1):
                    packed = packed + pltpu.roll(packed, n, 0)
                rows.append((c, packed))
            made.append((b, new, rows))
        for b, new, rows in made:
            for (a, c), value in new.items():
                plane[r, b // 2, a, c] = value
        start(r + 1, [off for off in far if not off[2]])
        for b, new, rows in made:
            for c, packed in rows:
                zrow[r, b // 2, c // 2] = packed

    def arrive(r):
        made = copies(r)
        for off in reversed(OFFSETS):
            pl.when(exists(back(off)))(made[off].wait_recv)

    def leave(r):
        made = copies(r)
        for off in OFFSETS:
            pl.when(exists(off))(made[off].wait_send)

    def edge(r, dz):
        def at(dx, dy):
            return zrecv[r, OFFSETS.index((dx, dy, dz))]

        def line(dx):
            return jnp.where(ymask[1], at(dx, 1), jnp.where(ymask[-1], at(dx, -1), at(dx, 0)))

        return jnp.where(xmask[1], line(1), jnp.where(xmask[-1], line(-1), line(0)))

    loads[0].wait()
    tiles = lax.fori_loop(
        0, 8, lambda x, t: pack(t, x, lambda a, b, c: adjs[0][a, b, c, x + 1, pl.ds(8, 8), :]), (zero, zero),
        unroll=8,
    )
    fill(0, tiles)
    pl.semaphore_wait(barrier, count)
    start(0, OFFSETS)

    for off in ((-1, 0, 0), (1, 0, 0)):

        @pl.when(jnp.logical_not(exists(off)))
        def _():
            part = 0 if off[0] < 0 else 9

            for adj in adjs:
                for b, c in PAIRS:
                    for tile in range(3):
                        adj[1 + off[0], b, c, part, pl.ds(8 * tile, 8), :] = zero

    for off in ((0, -1, 0), (0, 1, 0)):

        @pl.when(jnp.logical_not(exists(off)))
        def _():
            def clear(x, _):
                for adj in adjs:
                    for a, c in PAIRS:
                        adj[a, 1 + off[1], c, x, pl.ds(0 if off[1] < 0 else 16, 8), :] = zero
                return 0

            lax.fori_loop(0, 10, clear, 0)

    for k, off in enumerate(OFFSETS):
        if off[2]:

            @pl.when(jnp.logical_not(exists(back(off))))
            def _():
                for r in range(STEPS):
                    zrecv[r, k] = zero

    for t in (2, 1, 0):
        loads[1 + t].wait()

    def prepare(x, _):
        for t in range(STEPS):
            rho, mx, my, mz = f_moments(lambda a, b, c: pops[t][9 * a + 3 * b + c, x])
            flow[t][0, x] = rho
            flow[t][1, x] = mx / rho
            flow[t][2, x] = my / rho
            flow[t][3, x] = mz / rho
        return 0

    lax.fori_loop(0, 8, prepare, 0)
    loads[4].wait()
    loads[5].wait()

    for r in range(STEPS - 1):
        t = STEPS - 1 - r
        arrive(r)
        sides = edge(r, -1), edge(r, 1)

        outer_planes(r, t, sides)
        start(r + 1, [off for off in far if off[2]])

        def step(x, tiles):
            p = pull(slice_of(adjs[r], x), x, sides, lane)
            new = {}

            def store(a, b, c, value):
                new[a, b, c] = value
                adjs[r + 1][a, b, c, x + 1, pl.ds(8, 8), :] = value

            new_adjoint(p, terms(p, [flow[t][k, x] for k in (1, 2, 3)]), jnp.where(flu[x] == 1, por[x], 1.0), store)
            return pack(tiles, x, lambda a, b, c: new[a, b, c])

        fill(r + 1, lax.fori_loop(0, 8, step, (zero, zero), unroll=8))
        start(r + 1, near)

        def gradient(x, _):
            p = pull(slice_of(adjs[r], x), x, sides, lane)
            term = porosity_term(p, terms(p, [flow[t][k, x] for k in (1, 2, 3)]), flow[t][0, x], pops[t], x)
            term = jnp.where(flu[x] == 1, term, 0.0)
            acc[x] = term if r == 0 else acc[x] + term
            return 0

        lax.fori_loop(0, 8, gradient, 0)
        leave(r)

    leave(STEPS - 1)
    arrive(STEPS - 1)
    edges[0] = edge(STEPS - 1, -1)
    edges[1] = edge(STEPS - 1, 1)


def solution(mesh):
    sizes = tuple(mesh.shape[a] for a in AXES)
    f32 = jnp.float32
    vmem, tiles = pl.BlockSpec(memory_space=pltpu.VMEM), (8, 8, 128)
    between = (
        pltpu.VMEM((3, 3, 3, 10, 24, 128), f32),
        pltpu.VMEM((2, 8, 128), f32),
        pltpu.VMEM((27, *tiles), f32),
        pltpu.VMEM((4, *tiles), f32),
        pltpu.VMEM(tiles, f32),
        pltpu.VMEM(tiles, jnp.int32),
        pltpu.VMEM(tiles, f32),
    )
    exchange = pl.pallas_call(
        functools.partial(kernel, sizes),
        out_shape=between,
        in_specs=[pl.BlockSpec(memory_space=pltpu.HBM)] * 4,
        out_specs=[vmem] * len(between),
        scratch_shapes=[
            pltpu.VMEM((2, 3, 3, 3, 10, 24, 128), f32),
            pltpu.VMEM((2, 27, *tiles), f32),
            pltpu.VMEM((2, 4, *tiles), f32),
            pltpu.VMEM((STEPS, 2, 8, 128), f32),
            pltpu.VMEM((STEPS, 26, 8, 128), f32),
            pltpu.VMEM((2, 2, 3, 3, 8, 128), f32),
            pltpu.VMEM((2, 2, 2, 8, 128), f32),
            pltpu.SemaphoreType.DMA((6,)),
            pltpu.SemaphoreType.DMA((STEPS, 26)),
            pltpu.SemaphoreType.DMA((STEPS, 26)),
        ],
        compiler_params=pltpu.CompilerParams(
            collective_id=0, has_side_effects=True, vmem_limit_bytes=56 * 1024 * 1024
        ),
    )
    last = pl.pallas_call(
        last_kernel,
        out_shape=(jax.ShapeDtypeStruct((27, *tiles), f32), jax.ShapeDtypeStruct(tiles, f32)),
        in_specs=[vmem] * len(between),
        out_specs=[pl.BlockSpec(memory_space=pltpu.HBM)] * 2,
        scratch_shapes=[
            pltpu.VMEM((27, *tiles), f32),
            pltpu.VMEM(tiles, f32),
            pltpu.SemaphoreType.DMA((9,)),
        ],
        compiler_params=pltpu.CompilerParams(vmem_limit_bytes=48 * 1024 * 1024),
    )

    def local(saved, porosity, fluid, seed_adjoint):
        return last(*exchange(saved, porosity, fluid, seed_adjoint.reshape(3, 3, 3, 8, 8, 128)))

    return jax.shard_map(
        local,
        mesh=mesh,
        in_specs=(
            P(None, None, "gx", "gy", "gz"),
            P("gx", "gy", "gz"),
            P("gx", "gy", "gz"),
            P(None, "gx", "gy", "gz"),
        ),
        out_specs=(P(None, "gx", "gy", "gz"), P("gx", "gy", "gz")),
        check_vma=False,
    )
```
